256 devices in a mesh: lat: 32 (over z, x_lo, core), krylov: 8 (over x_hi, y).
Axes of the slice: x: 4 (x_hi: 2, x_lo: 2; x = x_hi * 2 + x_lo), y: 4, z: 8, core: 2. Of those that a mesh axis runs over, the one named last changes fastest.
Arguments:
- start_block: bfloat16 [32, 4, 16, 2, 400], P('lat'), may hold values from -6 to 6
- self_block: bfloat16 [32, 4, 2, 400, 400], P('lat'), may hold values from -1 to 1, as said below
- hop_links: bfloat16 [32, 4, 2, 2, 400, 400], P('lat'), may hold values from -0.078125 to 0.078125
- stored_vectors: bfloat16 [1024, 32, 4, 2, 400], P('krylov', 'lat'), may hold values from -0.01953125 to 0.01953125
Outputs:
- filtered_block: bfloat16 [32, 4, 16, 2, 400], P('lat')
- coefficients: float32 [1024, 2, 16], P('krylov')
The draws below stay inside these ranges and needn't reach their ends.
Inputs may be any that keep to these rules, and one draw needn't show every extreme that they name: `self_block`: each site's block is Hermitian: its real part is symmetric and its imaginary part antisymmetric.
All inputs are finite; a program needn't handle non-finite values.
Results may differ from the reference program's by a relative error of at most 0.024.
Values may be sent and summed in bfloat16 or wider, within the bound.
A program may use at most 128 MiB of HBM per device.

```python
import jax
import jax.numpy as jnp
from jax import lax

NB = 400
RHS = 16
DEG = 6
LX = 4
LT = 32
KRYLOV = 1024


def draw_self_block(key, part):
    key = jax.random.fold_in(key, 11)
    first_key, second_key, third_key = jax.random.split(key, 3)
    shape = (LT, LX, NB, NB)
    first = jax.random.truncated_normal(first_key, -4.0, 4.0, shape, jnp.float32)
    second = jax.random.truncated_normal(second_key, -4.0, 4.0, shape, jnp.float32)
    factor = 0.5 / NB ** 0.5
    real_part = 0.5 * factor * (first + jnp.swapaxes(first, -1, -2))
    imag_part = 0.5 * factor * (second - jnp.swapaxes(second, -1, -2))
    shifts = jax.random.uniform(third_key, (LT, LX, NB), jnp.float32, -0.5, 0.5)
    real_part = real_part + shifts[..., None] * jnp.eye(NB, dtype=jnp.float32)
    return jnp.stack([real_part, imag_part], axis=2).astype(jnp.bfloat16)


def level_of(rng, shape, cuts, smallest, top_value):
    level, own = 1.0, jax.random.fold_in(rng, 6)
    for axis_at, blocks in cuts:
        draws = jnp.exp(jax.random.uniform(jax.random.fold_in(own, axis_at), (blocks,), jnp.float32, smallest / len(cuts), top_value / len(cuts)))
        level = level * jnp.repeat(draws, shape[axis_at] // blocks).reshape([-1 if axis == axis_at else 1 for axis in range(len(shape))])
    return level


def normal_values(key, shape, deviation, reach, cuts=(), held_as=jnp.bfloat16):
    result = deviation * jax.random.normal(key, shape, jnp.float32)
    if cuts:
        result = result * level_of(key, shape, cuts, -0.22, 0.18)
    return jnp.clip(result, -reach, reach).astype(held_as)


def setup_inputs(seed: int = 0) -> dict:
    seeds = jax.random.split(jax.random.key(seed), 5)
    start_block = normal_values(seeds[0], (LT, LX, RHS, 2, NB), 1.0, 6.0, ((0, 32),))
    self_block = draw_self_block(jax.random.fold_in(seeds[4], 71), 0)
    hop_links = normal_values(seeds[2], (LT, LX, 2, 2, NB, NB), (16 * NB) ** -0.5, 0.078125, ((0, 32),))
    stored_vectors = normal_values(seeds[3], (KRYLOV, LT, LX, 2, NB), (LT * LX * 2 * NB) ** -0.5, 0.01953125, ((0, 8), (1, 32)))
    return dict(start_block=start_block, self_block=self_block, hop_links=hop_links, stored_vectors=stored_vectors)


CENTER = 0.25
HALF_WIDTH = 3.25


def forward_hop(link, vector):
    product = jnp.einsum("tsrcb,tsdab->tsrcda", vector.astype(jnp.float32), link.astype(jnp.float32))
    real_part = product[..., 0, 0, :] - product[..., 1, 1, :]
    imag_part = product[..., 1, 0, :] + product[..., 0, 1, :]
    return jnp.stack([real_part, imag_part], axis=3)


def adjoint_hop(link, vector):
    product = jnp.einsum("tsrcb,tsdba->tsrcda", vector.astype(jnp.float32), link.astype(jnp.float32))
    real_part = product[..., 0, 0, :] + product[..., 1, 1, :]
    imag_part = product[..., 1, 0, :] - product[..., 0, 1, :]
    return jnp.stack([real_part, imag_part], axis=3)


def operate(rounded, self_block, hop_links):
    x_links = hop_links[:, :, 0]
    t_links = hop_links[:, :, 1]
    total = forward_hop(self_block, rounded)
    total = total + forward_hop(x_links, jnp.roll(rounded, -1, axis=1))
    total = total + jnp.roll(adjoint_hop(x_links, rounded), 1, axis=1)
    total = total + forward_hop(t_links, jnp.roll(rounded, -1, axis=0))
    total = total + jnp.roll(adjoint_hop(t_links, rounded), 1, axis=0)
    return total


def chebyshev(start, self_block, hop_links):
    previous = start
    current = (operate(start.astype(jnp.bfloat16), self_block, hop_links) - CENTER * start) / HALF_WIDTH
    for degree_step in range(DEG - 1):
        image = operate(current.astype(jnp.bfloat16), self_block, hop_links)
        following = (2.0 / HALF_WIDTH) * (image - CENTER * current) - previous
        previous, current = current, following
    return current


def pairing(stored):
    count = stored.shape[0]
    flat = stored.reshape(count, -1)
    turned = jnp.stack([-stored[..., 1, :], stored[..., 0, :]], axis=3).reshape(count, -1)
    return flat, jnp.concatenate([flat, turned], axis=0)


def coefficient_terms(vectors_flat, block):
    rounded = block.astype(jnp.bfloat16)
    turned = jnp.stack([rounded[..., 1, :], -rounded[..., 0, :]], axis=3)
    joined = jnp.concatenate([rounded, turned], axis=2)
    rows = jnp.transpose(joined, (2, 0, 1, 3, 4)).reshape(joined.shape[2], -1)
    return lax.dot_general(vectors_flat, rows, (((1,), (1,)), ((), ())), preferred_element_type=jnp.float32)


def correction(paired_flat, coefs, block_shape):
    width = coefs.shape[1] // 2
    rounded = coefs.astype(jnp.bfloat16)
    stacked = jnp.concatenate([rounded[:, :width], rounded[:, width:]], axis=0)
    terms = lax.dot_general(paired_flat, stacked, (((0,), (0,)), ((), ())), preferred_element_type=jnp.float32)
    terms = terms.reshape(block_shape[0], block_shape[1], block_shape[3], block_shape[4], block_shape[2])
    return jnp.transpose(terms, (0, 1, 4, 2, 3))


def reference(start_block, self_block, hop_links, stored_vectors):
    block = chebyshev(start_block.astype(jnp.float32), self_block, hop_links)
    block = chebyshev(block, self_block, hop_links)
    vectors_flat, paired_flat = pairing(stored_vectors)
    total = jnp.zeros((stored_vectors.shape[0], 2 * block.shape[2]), jnp.float32)
    for pass_index in range(2):
        coefs = coefficient_terms(vectors_flat, block)
        total = total + coefs
        block = block - correction(paired_flat, coefs, block.shape)
    coefficients = total.reshape(stored_vectors.shape[0], 2, block.shape[2])
    return block.astype(jnp.bfloat16), coefficients
```

```python
import functools

import jax
import jax.numpy as jnp
from jax import lax
from jax.experimental import pallas as pl
from jax.experimental.pallas import tpu as pltpu
from jax.sharding import PartitionSpec as P

MESH = pl.DeviceIdType.MESH
BF16, F32 = jnp.bfloat16, jnp.float32

DEG = 6
CENTER = 0.25
HALF_WIDTH = 3.25

SITES, NB = 4, 400
QUARTER = 4
ROWS = 2 * QUARTER
FLAT = SITES * 2 * NB
GROUP = 128
CHIPS = 16


def dot(x, w):
    return lax.dot_general(x, w, (((1,), (0,)), ((), ())), preferred_element_type=F32)


def dot_t(x, w):
    return lax.dot_general(x, w, (((1,), (1,)), ((), ())), preferred_element_type=F32)


def turn(x):
    half = x.shape[0] // 2
    if x.shape[0] == ROWS:
        return jnp.concatenate([x[half:], -x[:half]], axis=0)
    return jnp.concatenate(
        [turn(x[i : i + ROWS]) for i in range(0, x.shape[0], ROWS)], axis=0
    )


def kernel(
    start_ref, self_hbm, hop_hbm, stored_hbm,
    out_ref, coef_ref,
    self_w, hop_w, ahead_w, stored,
    cur, prev, vsend, vrecv, psend, precv,
    asend, arecv, zbuf, dsend, drecv, ssend, srecv, fbuf, ebuf,
    load_sem, vs_sem, vr_sem, ps_sem, pr_sem, gs_sem, gr_sem,
    as_sem, ar_sem, zs_sem, zr_sem, ds_sem, dr_sem, ss_sem, sr_sem,
    fs_sem, fr_sem, es_sem, er_sem,
):
    lat, kry = lax.axis_index("lat"), lax.axis_index("krylov")
    y, h = lax.rem(kry, 4), kry // 4
    core, chip = lax.rem(lat, 2), lat // 2
    ahead = (lax.rem(lat + 1, 32), kry)
    behind = (lax.rem(lat + 31, 32), kry)
    partner = (chip * 2 + 1 - core, kry)
    sibling = (lat, (1 - h) * 4 + y)

    def ring(j):
        return lax.rem(y + j, 4)

    def along_y(j):
        return (lat, h * 4 + ring(j))

    def other_chip(j):
        return lax.rem(chip + j, CHIPS)

    barrier = pltpu.get_barrier_semaphore()
    greet = [ahead, behind, sibling]
    greet += [along_y(j) for j in (1, 2, 3)]
    greet += [(other_chip(j) * 2 + core, kry) for j in range(1, CHIPS)]
    for device in greet:
        pl.semaphore_signal(barrier, inc=1, device_id=device, device_id_type=MESH)

    def remote(src, dst, send_sem, recv_sem, device):
        return pltpu.make_async_remote_copy(
            src_ref=src, dst_ref=dst, send_sem=send_sem, recv_sem=recv_sem,
            device_id=device, device_id_type=MESH,
        )

    loads = [
        pltpu.make_async_copy(hop_hbm, hop_w, load_sem.at[0]),
        pltpu.make_async_copy(self_hbm, self_w, load_sem.at[1]),
        pltpu.make_async_copy(stored_hbm, stored.at[pl.ds(0, GROUP)], load_sem.at[2]),
    ]
    for load in loads:
        load.start()
    cur[...] = start_ref[...]
    prev[...] = start_ref[...]
    loads[0].wait()
    row = lax.broadcasted_iota(jnp.int32, (NB, NB), 0)
    col = lax.broadcasted_iota(jnp.int32, (NB, NB), 1)
    eye = (row == col).astype(BF16)

    def flip(site, carry):
        ahead_w[site, 0] = dot_t(eye, hop_w[site, 1, 0]).astype(BF16)
        ahead_w[site, 1] = (-dot_t(eye, hop_w[site, 1, 1])).astype(BF16)
        return carry

    lax.fori_loop(0, SITES, flip, 0)
    loads[1].wait()

    pl.semaphore_wait(barrier, len(greet))

    gathers = [
        remote(
            stored_hbm, stored.at[pl.ds(j * GROUP, GROUP)],
            gs_sem.at[j - 1], gr_sem.at[j - 1], along_y(j),
        )
        for j in (1, 2, 3)
    ]
    for gather in gathers:
        gather.start()

    def step(i, carry):
        p = lax.rem(i, 2)
        first = lax.rem(i, DEG) == 0
        scale = jnp.where(first, 1.0 / HALF_WIDTH, 2.0 / HALF_WIDTH).astype(F32)
        keep = jnp.where(first, 0.0, 1.0).astype(F32)
        x = cur[...]
        xb = x.astype(BF16)
        xt = turn(x).astype(BF16)
        vsend[...] = xb
        back = remote(vsend, vrecv.at[p], vs_sem.at[p], vr_sem.at[p], behind)
        back.start()
        parts = []
        for s in range(SITES):
            rows = slice(s * ROWS, s * ROWS + ROWS)
            parts.append(dot(xb[rows], hop_w[s, 1, 0]) + dot(xt[rows], hop_w[s, 1, 1]))
        psend[...] = jnp.concatenate(parts, axis=0).astype(BF16)
        forth = remote(psend, precv.at[p], ps_sem.at[p], pr_sem.at[p], ahead)
        forth.start()
        parts = []
        for s in range(SITES):
            rows = slice(s * ROWS, s * ROWS + ROWS)
            nxt = (s + 1) % SITES
            nrows = slice(nxt * ROWS, nxt * ROWS + ROWS)
            lst = (s - 1) % SITES
            lrows = slice(lst * ROWS, lst * ROWS + ROWS)
            total = dot(xb[rows], self_w[s, 0]) + dot(xt[rows], self_w[s, 1])
            total += dot(xb[lrows], hop_w[lst, 0, 0]) + dot(xt[lrows], hop_w[lst, 0, 1])
            total += dot_t(xb[nrows], hop_w[s, 0, 0]) - dot_t(xt[nrows], hop_w[s, 0, 1])
            parts.append(total)
        here = jnp.concatenate(parts, axis=0)
        base = scale * (here - CENTER * x) - keep * prev[...]
        back.wait_recv()
        vb = vrecv[p]
        vt = turn(vb.astype(F32)).astype(BF16)
        parts = []
        for s in range(SITES):
            rows = slice(s * ROWS, s * ROWS + ROWS)
            parts.append(dot(vb[rows], ahead_w[s, 0]) + dot(vt[rows], ahead_w[s, 1]))
        there = jnp.concatenate(parts, axis=0)
        forth.wait_recv()
        there = there + precv[p].astype(F32)
        prev[...] = x
        cur[...] = base + scale * there
        back.wait_send()
        forth.wait_send()
        return carry

    lax.fori_loop(0, 2 * DEG, step, 0)

    loads[2].wait()
    for gather in gathers:
        gather.wait()

    total = None
    for n in range(2):
        x = cur[...]
        xt = turn(x)
        pieces = []
        for s in range(SITES):
            rows = slice(s * ROWS, s * ROWS + ROWS)
            pieces += [x[rows], xt[rows]]
        flat = jnp.concatenate(pieces, axis=1).astype(BF16)
        part = dot_t(flat, stored[...])
        low, high = part[:, : 2 * GROUP], part[:, 2 * GROUP :]
        asend[n] = jnp.where(core == 0, high, low)
        cross = remote(asend.at[n], arecv.at[n], as_sem.at[n], ar_sem.at[n], partner)
        cross.start()
        mine = jnp.where(core == 0, low, high)
        cross.wait_recv()
        mine = mine + arecv[n]
        zbuf[n, chip] = jnp.concatenate(
            [mine[:, :GROUP], mine[:, GROUP:]], axis=0
        ).astype(BF16)
        sends = []
        for j in (8, 7, 9, 6, 10, 5, 11, 4, 12, 3, 13, 2, 14, 1, 15):
            sends.append(
                remote(
                    zbuf.at[n, chip], zbuf.at[n, chip], zs_sem.at[n, j], zr_sem.at[n, chip],
                    (other_chip(j) * 2 + core, kry),
                )
            )
        for send in sends:
            send.start()
        for j in range(1, CHIPS):
            source = other_chip(j)
            remote(
                zbuf.at[n, source], zbuf.at[n, source], zs_sem.at[n, j], zr_sem.at[n, source],
                (other_chip(j) * 2 + core, kry),
            ).wait_recv()
        summed = zbuf[n, 0].astype(F32)
        for q in range(1, CHIPS):
            summed = summed + zbuf[n, q].astype(F32)
        own = jnp.concatenate([summed[:ROWS], summed[ROWS:]], axis=1)
        dsend[n] = own
        cross_back = remote(dsend.at[n], drecv.at[n], ds_sem.at[n], dr_sem.at[n], partner)
        cross_back.start()
        cross_back.wait_recv()
        other = drecv[n]
        coef = jnp.concatenate(
            [jnp.where(core == 0, own, other), jnp.where(core == 0, other, own)], axis=1
        )
        total = coef if total is None else total + coef
        if n == 1:
            for j in range(4):
                ebuf[0, j] = total[:, j * GROUP : (j + 1) * GROUP]
            coef_sends = [
                remote(
                    ebuf.at[0, j], ebuf.at[1, j], es_sem.at[j - 1], er_sem.at[j - 1],
                    along_y(4 - j),
                )
                for j in (1, 2, 3)
            ]
            for send in coef_sends:
                send.start()
        spread = dot(coef.astype(BF16), stored[...])
        parts = []
        for s in range(SITES):
            at = s * 2 * NB
            parts.append(spread[:, at : at + NB] - turn(spread[:, at + NB : at + 2 * NB]))
        ssend[n] = jnp.concatenate(parts, axis=0).astype(BF16)
        pair = remote(ssend.at[n], srecv.at[n], ss_sem.at[n], sr_sem.at[n], sibling)
        pair.start()
        pair.wait_recv()
        cur[...] = x - (ssend[n].astype(F32) + srecv[n].astype(F32))
        cross.wait_send()
        for send in sends:
            send.wait_send()
        cross_back.wait_send()
        pair.wait_send()

    fbuf[y] = cur[...].astype(BF16)
    final = [
        remote(fbuf.at[y], fbuf.at[y], fs_sem.at[j - 1], fr_sem.at[j - 1], along_y(j))
        for j in (1, 2, 3)
    ]
    for send in final:
        send.start()
    for send in coef_sends:
        send.wait()
    coef_ref[y] = ebuf[0, 0]
    for j in (1, 2, 3):
        coef_ref[ring(j)] = ebuf[1, j]
    for j in (1, 2, 3):
        source = ring(4 - j)
        remote(
            fbuf.at[source], fbuf.at[source], fs_sem.at[j - 1], fr_sem.at[j - 1], along_y(j)
        ).wait_recv()
    for send in final:
        send.wait_send()
    out_ref[...] = fbuf[...]


def shards(start_block, self_block, hop_links, stored_vectors):
    y = lax.rem(lax.axis_index("krylov"), 4)
    mine = lax.dynamic_slice_in_dim(start_block[0], y * QUARTER, QUARTER, axis=1)
    mine = jnp.transpose(mine, (0, 2, 1, 3)).reshape(SITES * ROWS, NB).astype(F32)
    flat = stored_vectors.reshape(GROUP, FLAT)
    vmem, anywhere = pltpu.VMEM, pl.BlockSpec(memory_space=pl.ANY)
    here = pl.BlockSpec(memory_space=vmem)
    dma, block = pltpu.SemaphoreType.DMA, (SITES * ROWS, NB)
    out, coef = pl.pallas_call(
        kernel,
        out_shape=(
            jax.ShapeDtypeStruct((4,) + block, BF16),
            jax.ShapeDtypeStruct((4, ROWS, GROUP), F32),
        ),
        in_specs=[here, anywhere, anywhere, anywhere],
        out_specs=(here, here),
        scratch_shapes=[
            vmem((SITES, 2, NB, NB), BF16),
            vmem((SITES, 2, 2, NB, NB), BF16),
            vmem((SITES, 2, NB, NB), BF16),
            vmem((4 * GROUP, FLAT), BF16),
            vmem(block, F32),
            vmem(block, F32),
            vmem(block, BF16),
            vmem((2,) + block, BF16),
            vmem(block, BF16),
            vmem((2,) + block, BF16),
            vmem((2, ROWS, 2 * GROUP), F32),
            vmem((2, ROWS, 2 * GROUP), F32),
            vmem((2, CHIPS, 2 * ROWS, GROUP), BF16),
            vmem((2, ROWS, 2 * GROUP), F32),
            vmem((2, ROWS, 2 * GROUP), F32),
            vmem((2,) + block, BF16),
            vmem((2,) + block, BF16),
            vmem((4,) + block, BF16),
            vmem((2, 4, ROWS, GROUP), F32),
            dma((3,)),
            dma((2,)), dma((2,)), dma((2,)), dma((2,)),
            dma((3,)), dma((3,)),
            dma((2,)), dma((2,)),
            dma((2, CHIPS)), dma((2, CHIPS)),
            dma((2,)), dma((2,)), dma((2,)), dma((2,)),
            dma((3,)), dma((3,)), dma((3,)), dma((3,)),
        ],
        compiler_params=pltpu.CompilerParams(
            collective_id=0, has_side_effects=True, vmem_limit_bytes=48 * 2**20
        ),
    )(mine, self_block[0], hop_links[0], flat)
    out = out.reshape(4, SITES, 2, QUARTER, NB)
    out = jnp.transpose(out, (1, 0, 3, 2, 4)).reshape(1, SITES, 16, 2, NB)
    coef = coef.reshape(4, 2, QUARTER, GROUP)
    coef = jnp.transpose(coef, (3, 1, 0, 2)).reshape(GROUP, 2, 16)
    return out, coef


def solution(mesh):
    placed = (
        P("lat", None, None, None, None),
        P("lat", None, None, None, None),
        P("lat", None, None, None, None, None),
        P("krylov", "lat", None, None, None),
    )
    return jax.shard_map(
        shards,
        mesh=mesh,
        in_specs=placed,
        out_specs=(P("lat", None, None, None, None), P("krylov", None, None)),
        check_vma=False,
    )
```

```python
import functools

import jax
import jax.numpy as jnp
from jax import lax
from jax.experimental import pallas as pl
from jax.experimental.pallas import tpu as pltpu
from jax.sharding import PartitionSpec as P

MESH = pl.DeviceIdType.MESH
BF16, F32 = jnp.bfloat16, jnp.float32

DEG = 6
CENTER = 0.25
HALF_WIDTH = 3.25

SITES, NB = 4, 400
QUARTER = 4
ROWS = 2 * QUARTER
FLAT = SITES * 2 * NB
GROUP = 128
CHIPS = 16


def dot(x, w):
    return lax.dot_general(x, w, (((1,), (0,)), ((), ())), preferred_element_type=F32)


def dot_t(x, w):
    return lax.dot_general(x, w, (((1,), (1,)), ((), ())), preferred_element_type=F32)


def turn(x):
    half = x.shape[0] // 2
    if x.shape[0] == ROWS:
        return jnp.concatenate([x[half:], -x[:half]], axis=0)
    return jnp.concatenate(
        [turn(x[i : i + ROWS]) for i in range(0, x.shape[0], ROWS)], axis=0
    )


def kernel(
    start_ref, self_hbm, hop_hbm, stored_hbm,
    out_ref, coef_ref,
    self_w, space_w, time_w, ahead_w, stored,
    cur, prev, bsend, vrecv, psend, precv,
    asend, arecv, zbuf, dsend, drecv, ssend, srecv, fbuf, ebuf,
    load_sem, vs_sem, vr_sem, ps_sem, pr_sem, gs_sem, gr_sem,
    as_sem, ar_sem, zs_sem, zr_sem, ds_sem, dr_sem, ss_sem, sr_sem,
    fs_sem, fr_sem, es_sem, er_sem,
):
    lat, kry = lax.axis_index("lat"), lax.axis_index("krylov")
    y, h = lax.rem(kry, 4), kry // 4
    core, chip = lax.rem(lat, 2), lat // 2
    ahead = (lax.rem(lat + 1, 32), kry)
    behind = (lax.rem(lat + 31, 32), kry)
    partner = (chip * 2 + 1 - core, kry)
    sibling = (lat, (1 - h) * 4 + y)

    def ring(j):
        return lax.rem(y + j, 4)

    def along_y(j):
        return (lat, h * 4 + ring(j))

    def other_chip(j):
        return lax.rem(chip + j, CHIPS)

    barrier = pltpu.get_barrier_semaphore()
    greet = [ahead, behind, sibling]
    greet += [along_y(j) for j in (1, 2, 3)]
    greet += [(other_chip(j) * 2 + core, kry) for j in range(1, CHIPS)]
    for device in greet:
        pl.semaphore_signal(barrier, inc=1, device_id=device, device_id_type=MESH)

    def remote(src, dst, send_sem, recv_sem, device):
        return pltpu.make_async_remote_copy(
            src_ref=src, dst_ref=dst, send_sem=send_sem, recv_sem=recv_sem,
            device_id=device, device_id_type=MESH,
        )

    loads = [
        pltpu.make_async_copy(hop_hbm.at[:, 1], time_w, load_sem.at[0]),
        pltpu.make_async_copy(self_hbm, self_w, load_sem.at[1]),
        pltpu.make_async_copy(hop_hbm.at[:, 0], space_w, load_sem.at[2]),
        pltpu.make_async_copy(stored_hbm, stored.at[:, pl.ds(0, GROUP)], load_sem.at[3]),
    ]
    for load in loads:
        load.start()
    cur[...] = start_ref[...]
    prev[...] = start_ref[...]
    psend[1] = jnp.zeros_like(psend[1])
    loads[0].wait()

    pl.semaphore_wait(barrier, len(greet))

    gathers = [
        remote(
            stored_hbm, stored.at[:, pl.ds(j * GROUP, GROUP)],
            gs_sem.at[j - 1], gr_sem.at[j - 1], along_y(j),
        )
        for j in (1, 2, 3)
    ]

    def to_behind(slot):
        return remote(bsend, vrecv.at[slot], vs_sem, vr_sem.at[slot], behind)

    even, odd = core == 0, core == 1

    @pl.when(even)
    def _():
        bsend[...] = cur[...].astype(BF16)
        to_behind(0).start()

    def factor(i):
        first = lax.rem(i, DEG) == 0
        return jnp.where(first, 1.0 / HALF_WIDTH, 2.0 / HALF_WIDTH).astype(F32)

    def step(i, carry):
        p, slot = lax.rem(i, 2), lax.rem(i, 3)
        scale = factor(i)
        keep = jnp.where(lax.rem(i, DEG) == 0, 0.0, 1.0).astype(F32)
        x = cur[...]
        xb = x.astype(BF16)
        xt = turn(x).astype(BF16)

        @pl.when(odd)
        def _():
            bsend[...] = xb
            to_behind(slot).start()

        parts = []
        for s in range(SITES):
            rows = slice(s * ROWS, s * ROWS + ROWS)
            parts.append(dot(xb[rows], time_w[s, 0]) + dot(xt[rows], time_w[s, 1]))
        psend[p] = jnp.concatenate(parts, axis=0).astype(BF16)
        forth = remote(psend.at[p], precv.at[slot], ps_sem, pr_sem.at[slot], ahead)
        forth.start()

        @pl.when(i == 0)
        def _():
            for gather in gathers:
                gather.start()
            row = lax.broadcasted_iota(jnp.int32, (NB, NB), 0)
            col = lax.broadcasted_iota(jnp.int32, (NB, NB), 1)
            eye = (row == col).astype(BF16)

            def flip(site, carry):
                ahead_w[site, 0] = dot_t(eye, time_w[site, 0]).astype(BF16)
                ahead_w[site, 1] = (-dot_t(eye, time_w[site, 1])).astype(BF16)
                return carry

            lax.fori_loop(0, SITES, flip, 0)
            loads[1].wait()
            loads[2].wait()

        parts = []
        for s in range(SITES):
            rows = slice(s * ROWS, s * ROWS + ROWS)
            nxt = (s + 1) % SITES
            nrows = slice(nxt * ROWS, nxt * ROWS + ROWS)
            lst = (s - 1) % SITES
            lrows = slice(lst * ROWS, lst * ROWS + ROWS)
            total = dot(xb[rows], self_w[s, 0]) + dot(xt[rows], self_w[s, 1])
            total += dot(xb[lrows], space_w[lst, 0]) + dot(xt[lrows], space_w[lst, 1])
            total += dot_t(xb[nrows], space_w[s, 0]) - dot_t(xt[nrows], space_w[s, 1])
            parts.append(total)
        here = jnp.concatenate(parts, axis=0)
        base = scale * (here - CENTER * x) - keep * prev[...]
        to_behind(slot).wait_recv()
        known = jnp.where(odd, factor(i + DEG - 1), 0.0) * psend[1 - p].astype(F32)
        va = vrecv[slot].astype(F32) + known
        vb, vt = va.astype(BF16), turn(va).astype(BF16)
        parts = []
        for s in range(SITES):
            rows = slice(s * ROWS, s * ROWS + ROWS)
            parts.append(dot(vb[rows], ahead_w[s, 0]) + dot(vt[rows], ahead_w[s, 1]))
        base = base + scale * jnp.concatenate(parts, axis=0)
        to_behind(slot).wait_send()

        @pl.when(jnp.logical_and(even, i < 2 * DEG - 1))
        def _():
            bsend[...] = base.astype(BF16)
            to_behind(lax.rem(i + 1, 3)).start()

        forth.wait_recv()
        prev[...] = x
        cur[...] = base + scale * precv[slot].astype(F32)
        forth.wait_send()
        return carry

    lax.fori_loop(0, 2 * DEG, step, 0)

    loads[3].wait()
    for gather in gathers:
        gather.wait()

    my_half = pl.ds(pl.multiple_of(core * 2 * GROUP, 2 * GROUP), 2 * GROUP)
    its_half = pl.ds(pl.multiple_of((1 - core) * 2 * GROUP, 2 * GROUP), 2 * GROUP)
    mine_total = other_total = None
    for n in range(2):
        x = cur[...]
        xt = turn(x)
        pieces = []
        for s in range(SITES):
            rows = slice(s * ROWS, s * ROWS + ROWS)
            pieces += [x[rows], xt[rows]]
        pieces = [piece.astype(BF16) for piece in pieces]

        def project(half):
            total = None
            for q, piece in enumerate(pieces):
                term = dot(piece, stored[q * NB : (q + 1) * NB, half])
                total = term if total is None else total + term
            return total

        def spread(coef, half):
            coef = coef.astype(BF16)
            parts = []
            for s in range(SITES):
                at = s * 2 * NB
                real = dot_t(coef, stored[at : at + NB, half])
                imag = dot_t(coef, stored[at + NB : at + 2 * NB, half])
                parts.append(real - turn(imag))
            return jnp.concatenate(parts, axis=0)

        asend[n] = project(its_half)
        cross = remote(asend.at[n], arecv.at[n], as_sem.at[n], ar_sem.at[n], partner)
        cross.start()
        mine = project(my_half)
        cross.wait_recv()
        mine = mine + arecv[n]
        zbuf[n, chip] = jnp.concatenate(
            [mine[:, :GROUP], mine[:, GROUP:]], axis=0
        ).astype(BF16)
        sends = []
        for j in (8, 7, 9, 6, 10, 5, 11, 4, 12, 3, 13, 2, 14, 1, 15):
            sends.append(
                remote(
                    zbuf.at[n, chip], zbuf.at[n, chip], zs_sem.at[n, j], zr_sem.at[n, chip],
                    (other_chip(j) * 2 + core, kry),
                )
            )
        for send in sends:
            send.start()
        for j in range(1, CHIPS):
            source = other_chip(j)
            remote(
                zbuf.at[n, source], zbuf.at[n, source], zs_sem.at[n, j], zr_sem.at[n, source],
                (other_chip(j) * 2 + core, kry),
            ).wait_recv()
        summed = zbuf[n, 0].astype(F32)
        for q in range(1, CHIPS):
            summed = summed + zbuf[n, q].astype(F32)
        own = jnp.concatenate([summed[:ROWS], summed[ROWS:]], axis=1)
        dsend[n] = own
        cross_back = remote(dsend.at[n], drecv.at[n], ds_sem.at[n], dr_sem.at[n], partner)
        cross_back.start()
        change = spread(own, my_half)
        cross_back.wait_recv()
        other = drecv[n]
        mine_total = own if n == 0 else mine_total + own
        other_total = other if n == 0 else other_total + other
        if n == 1:
            low = jnp.where(even, mine_total, other_total)
            high = jnp.where(even, other_total, mine_total)
            ebuf[0, 0], ebuf[0, 1] = low[:, :GROUP], low[:, GROUP:]
            ebuf[0, 2], ebuf[0, 3] = high[:, :GROUP], high[:, GROUP:]
            coef_sends = [
                remote(
                    ebuf.at[0, j], ebuf.at[1, y], es_sem.at[j - 1], er_sem.at[j - 1],
                    along_y(4 - j),
                )
                for j in (1, 2, 3)
            ]
            for send in coef_sends:
                send.start()
        change = change + spread(other, its_half)
        ssend[n] = change.astype(BF16)
        pair = remote(ssend.at[n], srecv.at[n], ss_sem.at[n], sr_sem.at[n], sibling)
        pair.start()
        pair.wait_recv()
        cur[...] = x - (ssend[n].astype(F32) + srecv[n].astype(F32))
        cross.wait_send()
        for send in sends:
            send.wait_send()
        cross_back.wait_send()
        pair.wait_send()

    fbuf[y] = cur[...].astype(BF16)
    final = [
        remote(fbuf.at[y], fbuf.at[y], fs_sem.at[j - 1], fr_sem.at[j - 1], along_y(j))
        for j in (1, 2, 3)
    ]
    for send in final:
        send.start()
    ebuf[1, y] = ebuf[0, 0]
    for j in (1, 2, 3):
        source = ring(j)
        remote(
            ebuf.at[0, j], ebuf.at[1, source], es_sem.at[j - 1], er_sem.at[j - 1], along_y(4 - j)
        ).wait()
    for part in range(2):
        rows = slice(part * QUARTER, (part + 1) * QUARTER)
        coef_ref[part] = jnp.concatenate([ebuf[1, q, rows] for q in range(4)], axis=0)
    for j in (1, 2, 3):
        source = ring(4 - j)
        remote(
            fbuf.at[source], fbuf.at[source], fs_sem.at[j - 1], fr_sem.at[j - 1], along_y(j)
        ).wait_recv()
    for send in final:
        send.wait_send()
    out_ref[...] = fbuf[...]


def shards(start_block, self_block, hop_links, stored_vectors):
    y = lax.rem(lax.axis_index("krylov"), 4)
    mine = lax.dynamic_slice_in_dim(start_block[0], y * QUARTER, QUARTER, axis=1)
    mine = jnp.transpose(mine, (0, 2, 1, 3)).reshape(SITES * ROWS, NB).astype(F32)
    flat = jnp.transpose(stored_vectors.reshape(GROUP, FLAT))
    vmem, anywhere = pltpu.VMEM, pl.BlockSpec(memory_space=pltpu.HBM)
    here = pl.BlockSpec(memory_space=vmem)
    dma, block = pltpu.SemaphoreType.DMA, (SITES * ROWS, NB)
    out, coef = pl.pallas_call(
        kernel,
        out_shape=(
            jax.ShapeDtypeStruct((4,) + block, BF16),
            jax.ShapeDtypeStruct((2, 16, GROUP), F32),
        ),
        in_specs=[here, anywhere, anywhere, anywhere],
        out_specs=(here, here),
        scratch_shapes=[
            vmem((SITES, 2, NB, NB), BF16),
            vmem((SITES, 2, NB, NB), BF16),
            vmem((SITES, 2, NB, NB), BF16),
            vmem((SITES, 2, NB, NB), BF16),
            vmem((FLAT, 4 * GROUP), BF16),
            vmem(block, F32),
            vmem(block, F32),
            vmem(block, BF16),
            vmem((3,) + block, BF16),
            vmem((2,) + block, BF16),
            vmem((3,) + block, BF16),
            vmem((2, ROWS, 2 * GROUP), F32),
            vmem((2, ROWS, 2 * GROUP), F32),
            vmem((2, CHIPS, 2 * ROWS, GROUP), BF16),
            vmem((2, ROWS, 2 * GROUP), F32),
            vmem((2, ROWS, 2 * GROUP), F32),
            vmem((2,) + block, BF16),
            vmem((2,) + block, BF16),
            vmem((4,) + block, BF16),
            vmem((2, 4, ROWS, GROUP), F32),
            dma((4,)),
            dma, dma((3,)), dma, dma((3,)),
            dma((3,)), dma((3,)),
            dma((2,)), dma((2,)),
            dma((2, CHIPS)), dma((2, CHIPS)),
            dma((2,)), dma((2,)), dma((2,)), dma((2,)),
            dma((3,)), dma((3,)), dma((3,)), dma((3,)),
        ],
        compiler_params=pltpu.CompilerParams(
            collective_id=0, has_side_effects=True, vmem_limit_bytes=56 * 2**20
        ),
    )(mine, self_block[0], hop_links[0], flat)
    out = out.reshape(4, SITES, 2, QUARTER, NB)
    out = jnp.transpose(out, (1, 0, 3, 2, 4)).reshape(1, SITES, 16, 2, NB)
    return out, jnp.transpose(coef, (2, 0, 1))


def solution(mesh):
    placed = (
        P("lat", None, None, None, None),
        P("lat", None, None, None, None),
        P("lat", None, None, None, None, None),
        P("krylov", "lat", None, None, None),
    )
    return jax.shard_map(
        shards,
        mesh=mesh,
        in_specs=placed,
        out_specs=(P("lat", None, None, None, None), P("krylov", None, None)),
        check_vma=False,
    )
```

```python
import functools

import jax
import jax.numpy as jnp
from jax import lax
from jax.experimental import pallas as pl
from jax.experimental.pallas import tpu as pltpu
from jax.sharding import PartitionSpec as P

MESH = pl.DeviceIdType.MESH
BF16, F32 = jnp.bfloat16, jnp.float32

DEG = 6
CENTER = 0.25
HALF_WIDTH = 3.25

SITES, NB = 4, 400
QUARTER = 4
ROWS = 2 * QUARTER
FLAT = SITES * 2 * NB
GROUP = 128
CHIPS = 16


def dot(x, w):
    return lax.dot_general(x, w, (((1,), (0,)), ((), ())), preferred_element_type=F32)


def dot_t(x, w):
    return lax.dot_general(x, w, (((1,), (1,)), ((), ())), preferred_element_type=F32)


def turn(x):
    half = x.shape[0] // 2
    if x.shape[0] == ROWS:
        return jnp.concatenate([x[half:], -x[:half]], axis=0)
    return jnp.concatenate(
        [turn(x[i : i + ROWS]) for i in range(0, x.shape[0], ROWS)], axis=0
    )


def kernel(
    start_hbm, self_hbm, hop_hbm, stored_hbm,
    out_ref, coef_ref,
    start, self_w, space_w, time_w, ahead_w, stored,
    cur, prev, bsend, vrecv, psend, precv,
    asend, arecv, zbuf, dsend, drecv, ssend, srecv, fbuf, ebuf,
    load_sem, vs_sem, vr_sem, ps_sem, pr_sem, gs_sem, gr_sem,
    as_sem, ar_sem, zs_sem, zr_sem, ds_sem, dr_sem, ss_sem, sr_sem,
    fs_sem, fr_sem, es_sem, er_sem, word_sem,
):
    lat, kry = lax.axis_index("lat"), lax.axis_index("krylov")
    y, h = lax.rem(kry, 4), kry // 4
    core, chip = lax.rem(lat, 2), lat // 2
    ahead = (lax.rem(lat + 1, 32), kry)
    behind = (lax.rem(lat + 31, 32), kry)
    partner = (chip * 2 + 1 - core, kry)
    sibling = (lat, (1 - h) * 4 + y)

    def ring(j):
        return lax.rem(y + j, 4)

    def along_y(j):
        return (lat, h * 4 + ring(j))

    def other_chip(j):
        return lax.rem(chip + j, CHIPS)

    barrier = pltpu.get_barrier_semaphore()
    greet = [ahead, behind, sibling]
    greet += [along_y(j) for j in (1, 2, 3)]
    beside_z = [(other_chip(j) * 2 + core, kry) for j in (2, CHIPS - 2)]
    greet += beside_z
    for device in greet:
        pl.semaphore_signal(barrier, inc=1, device_id=device, device_id_type=MESH)

    def remote(src, dst, send_sem, recv_sem, device):
        return pltpu.make_async_remote_copy(
            src_ref=src, dst_ref=dst, send_sem=send_sem, recv_sem=recv_sem,
            device_id=device, device_id_type=MESH,
        )

    loads = [
        pltpu.make_async_copy(hop_hbm.at[:, 1], time_w, load_sem.at[0]),
        pltpu.make_async_copy(self_hbm, self_w, load_sem.at[1]),
        pltpu.make_async_copy(hop_hbm.at[:, 0], space_w, load_sem.at[2]),
        pltpu.make_async_copy(stored_hbm, stored.at[:, pl.ds(0, GROUP)], load_sem.at[3]),
        pltpu.make_async_copy(
            start_hbm.at[:, pl.ds(y * QUARTER, QUARTER)], start, load_sem.at[4]
        ),
    ]
    for q in (4, 0, 1, 2, 3):
        loads[q].start()
    loads[4].wait()
    block = start[...].astype(F32)
    block = jnp.concatenate(
        [block[s, r, c : c + 1] for s in range(SITES) for c in range(2) for r in range(QUARTER)],
        axis=0,
    )
    cur[...] = block
    prev[...] = block
    psend[1] = jnp.zeros_like(psend[1])
    loads[0].wait()

    def flip(site, carry):
        ahead_w[site, 0] = jnp.transpose(time_w[site, 0])
        ahead_w[site, 1] = -jnp.transpose(time_w[site, 1])
        return carry

    lax.fori_loop(0, SITES, flip, 0)
    pl.semaphore_wait(barrier, len(greet))

    gathers = [
        remote(
            stored_hbm, stored.at[:, pl.ds(j * GROUP, GROUP)],
            gs_sem.at[j - 1], gr_sem.at[j - 1], along_y(j),
        )
        for j in (1, 2, 3)
    ]

    def to_behind(slot):
        return remote(bsend, vrecv.at[slot], vs_sem, vr_sem.at[slot], behind)

    even, odd = core == 0, core == 1

    @pl.when(even)
    def _():
        bsend[...] = cur[...].astype(BF16)
        to_behind(0).start()

    def factor(i):
        first = lax.rem(i, DEG) == 0
        return jnp.where(first, 1.0 / HALF_WIDTH, 2.0 / HALF_WIDTH).astype(F32)

    def meet(i):
        for turn_at in range(5):

            @pl.when(i == 2 * turn_at + 2)
            def _():
                if turn_at > 0:
                    pl.semaphore_wait(word_sem.at[turn_at - 1, 0], 1)
                    pl.semaphore_wait(word_sem.at[turn_at - 1, 1], 1)
                if turn_at < 4:
                    for q, device in enumerate(beside_z):
                        pl.semaphore_signal(
                            word_sem.at[turn_at, q], inc=1, device_id=device, device_id_type=MESH
                        )

    def step(i, carry):
        p, slot = lax.rem(i, 2), lax.rem(i, 3)
        scale = factor(i)
        keep = jnp.where(lax.rem(i, DEG) == 0, 0.0, 1.0).astype(F32)
        x = cur[...]
        xb = x.astype(BF16)
        xt = turn(x).astype(BF16)

        @pl.when(odd)
        def _():
            bsend[...] = xb
            to_behind(slot).start()

        parts = []
        for s in range(SITES):
            rows = slice(s * ROWS, s * ROWS + ROWS)
            parts.append(dot(xb[rows], time_w[s, 0]) + dot(xt[rows], time_w[s, 1]))
        psend[p] = jnp.concatenate(parts, axis=0).astype(BF16)
        forth = remote(psend.at[p], precv.at[slot], ps_sem, pr_sem.at[slot], ahead)
        forth.start()
        meet(i)

        @pl.when(i == 0)
        def _():
            for gather in gathers:
                gather.start()
            loads[1].wait()
            loads[2].wait()

        parts = []
        for s in range(SITES):
            rows = slice(s * ROWS, s * ROWS + ROWS)
            nxt = (s + 1) % SITES
            nrows = slice(nxt * ROWS, nxt * ROWS + ROWS)
            lst = (s - 1) % SITES
            lrows = slice(lst * ROWS, lst * ROWS + ROWS)
            total = dot(xb[rows], self_w[s, 0]) + dot(xt[rows], self_w[s, 1])
            total += dot(xb[lrows], space_w[lst, 0]) + dot(xt[lrows], space_w[lst, 1])
            total += dot_t(xb[nrows], space_w[s, 0]) - dot_t(xt[nrows], space_w[s, 1])
            parts.append(total)
        here = jnp.concatenate(parts, axis=0)
        base = scale * (here - CENTER * x) - keep * prev[...]
        to_behind(slot).wait_recv()
        known = jnp.where(odd, factor(i + DEG - 1), 0.0) * psend[1 - p].astype(F32)
        va = vrecv[slot].astype(F32) + known
        vb, vt = va.astype(BF16), turn(va).astype(BF16)
        parts = []
        for s in range(SITES):
            rows = slice(s * ROWS, s * ROWS + ROWS)
            parts.append(dot(vb[rows], ahead_w[s, 0]) + dot(vt[rows], ahead_w[s, 1]))
        base = base + scale * jnp.concatenate(parts, axis=0)
        to_behind(slot).wait_send()

        @pl.when(jnp.logical_and(even, i < 2 * DEG - 1))
        def _():
            bsend[...] = base.astype(BF16)
            to_behind(lax.rem(i + 1, 3)).start()

        forth.wait_recv()
        prev[...] = x
        cur[...] = base + scale * precv[slot].astype(F32)
        forth.wait_send()
        return carry

    lax.fori_loop(0, 2 * DEG, step, 0)

    loads[3].wait()
    for gather in gathers:
        gather.wait()

    my_half = pl.ds(pl.multiple_of(core * 2 * GROUP, 2 * GROUP), 2 * GROUP)
    its_half = pl.ds(pl.multiple_of((1 - core) * 2 * GROUP, 2 * GROUP), 2 * GROUP)
    mine_total = other_total = None
    for n in range(2):
        x = cur[...]
        xt = turn(x)
        pieces = []
        for s in range(SITES):
            rows = slice(s * ROWS, s * ROWS + ROWS)
            pieces += [x[rows], xt[rows]]
        pieces = [piece.astype(BF16) for piece in pieces]

        def project(half):
            total = None
            for q, piece in enumerate(pieces):
                term = dot(piece, stored[q * NB : (q + 1) * NB, half])
                total = term if total is None else total + term
            return total

        def spread(coef, half):
            coef = coef.astype(BF16)
            parts = []
            for s in range(SITES):
                at = s * 2 * NB
                real = dot_t(coef, stored[at : at + NB, half])
                imag = dot_t(coef, stored[at + NB : at + 2 * NB, half])
                parts.append(real - turn(imag))
            return jnp.concatenate(parts, axis=0)

        asend[n] = project(its_half)
        cross = remote(asend.at[n], arecv.at[n], as_sem.at[n], ar_sem.at[n], partner)
        cross.start()
        mine = project(my_half)
        cross.wait_recv()
        mine = mine + arecv[n]
        zbuf[n, chip] = jnp.concatenate(
            [mine[:, :GROUP], mine[:, GROUP:]], axis=0
        ).astype(BF16)
        sends = []
        for j in (8, 7, 9, 6, 10, 5, 11, 4, 12, 3, 13, 2, 14, 1, 15):
            sends.append(
                remote(
                    zbuf.at[n, chip], zbuf.at[n, chip], zs_sem.at[n, j], zr_sem.at[n, chip],
                    (other_chip(j) * 2 + core, kry),
                )
            )
        for send in sends:
            send.start()
        for j in range(1, CHIPS):
            source = other_chip(j)
            remote(
                zbuf.at[n, source], zbuf.at[n, source], zs_sem.at[n, j], zr_sem.at[n, source],
                (other_chip(j) * 2 + core, kry),
            ).wait_recv()
        summed = zbuf[n, 0].astype(F32)
        for q in range(1, CHIPS):
            summed = summed + zbuf[n, q].astype(F32)
        own = jnp.concatenate([summed[:ROWS], summed[ROWS:]], axis=1)
        dsend[n] = own
        cross_back = remote(dsend.at[n], drecv.at[n], ds_sem.at[n], dr_sem.at[n], partner)
        cross_back.start()
        change = spread(own, my_half)
        cross_back.wait_recv()
        other = drecv[n]
        mine_total = own if n == 0 else mine_total + own
        other_total = other if n == 0 else other_total + other
        if n == 1:
            low = jnp.where(even, mine_total, other_total)
            high = jnp.where(even, other_total, mine_total)
            ebuf[0, 0], ebuf[0, 1] = low[:, :GROUP], low[:, GROUP:]
            ebuf[0, 2], ebuf[0, 3] = high[:, :GROUP], high[:, GROUP:]
            coef_sends = [
                remote(
                    ebuf.at[0, j], ebuf.at[1, y], es_sem.at[j - 1], er_sem.at[j - 1],
                    along_y(4 - j),
                )
                for j in (1, 2, 3)
            ]
            for send in coef_sends:
                send.start()
        change = change + spread(other, its_half)
        ssend[n] = change.astype(BF16)
        pair = remote(ssend.at[n], srecv.at[n], ss_sem.at[n], sr_sem.at[n], sibling)
        pair.start()
        pair.wait_recv()
        cur[...] = x - (ssend[n].astype(F32) + srecv[n].astype(F32))
        cross.wait_send()
        for send in sends:
            send.wait_send()
        cross_back.wait_send()
        pair.wait_send()

    fbuf[y] = cur[...].astype(BF16)
    final = [
        remote(fbuf.at[y], fbuf.at[y], fs_sem.at[j - 1], fr_sem.at[j - 1], along_y(j))
        for j in (1, 2, 3)
    ]
    for send in final:
        send.start()
    ebuf[1, y] = ebuf[0, 0]
    for j in (1, 2, 3):
        source = ring(j)
        remote(
            ebuf.at[0, j], ebuf.at[1, source], es_sem.at[j - 1], er_sem.at[j - 1], along_y(4 - j)
        ).wait()
    for part in range(2):
        rows = slice(part * QUARTER, (part + 1) * QUARTER)
        coef_ref[part] = jnp.concatenate([ebuf[1, q, rows] for q in range(4)], axis=0)
    for j in (1, 2, 3):
        source = ring(4 - j)
        remote(
            fbuf.at[source], fbuf.at[source], fs_sem.at[j - 1], fr_sem.at[j - 1], along_y(j)
        ).wait_recv()
    for send in final:
        send.wait_send()
    out_ref[...] = fbuf[...]


def shards(start_block, self_block, hop_links, stored_vectors):
    flat = jnp.transpose(stored_vectors.reshape(GROUP, FLAT))
    vmem, anywhere = pltpu.VMEM, pl.BlockSpec(memory_space=pltpu.HBM)
    here = pl.BlockSpec(memory_space=vmem)
    dma, block = pltpu.SemaphoreType.DMA, (SITES * ROWS, NB)
    out, coef = pl.pallas_call(
        kernel,
        out_shape=(
            jax.ShapeDtypeStruct((4,) + block, BF16),
            jax.ShapeDtypeStruct((2, 16, GROUP), F32),
        ),
        in_specs=[anywhere] * 4,
        out_specs=(here, here),
        scratch_shapes=[
            vmem((SITES, QUARTER, 2, NB), BF16),
            vmem((SITES, 2, NB, NB), BF16),
            vmem((SITES, 2, NB, NB), BF16),
            vmem((SITES, 2, NB, NB), BF16),
            vmem((SITES, 2, NB, NB), BF16),
            vmem((FLAT, 4 * GROUP), BF16),
            vmem(block, F32),
            vmem(block, F32),
            vmem(block, BF16),
            vmem((3,) + block, BF16),
            vmem((2,) + block, BF16),
            vmem((3,) + block, BF16),
            vmem((2, ROWS, 2 * GROUP), F32),
            vmem((2, ROWS, 2 * GROUP), F32),
            vmem((2, CHIPS, 2 * ROWS, GROUP), BF16),
            vmem((2, ROWS, 2 * GROUP), F32),
            vmem((2, ROWS, 2 * GROUP), F32),
            vmem((2,) + block, BF16),
            vmem((2,) + block, BF16),
            vmem((4,) + block, BF16),
            vmem((2, 4, ROWS, GROUP), F32),
            dma((5,)),
            dma, dma((3,)), dma, dma((3,)),
            dma((3,)), dma((3,)),
            dma((2,)), dma((2,)),
            dma((2, CHIPS)), dma((2, CHIPS)),
            dma((2,)), dma((2,)), dma((2,)), dma((2,)),
            dma((3,)), dma((3,)), dma((3,)), dma((3,)),
            pltpu.SemaphoreType.REGULAR((4, 2)),
        ],
        compiler_params=pltpu.CompilerParams(
            collective_id=0, has_side_effects=True, vmem_limit_bytes=55000 * 2**10
        ),
    )(start_block[0], self_block[0], hop_links[0], flat)
    out = out.reshape(4, SITES, 2, QUARTER, NB)
    out = jnp.transpose(out, (1, 0, 3, 2, 4)).reshape(1, SITES, 16, 2, NB)
    return out, jnp.transpose(coef, (2, 0, 1))


def solution(mesh):
    placed = (
        P("lat", None, None, None, None),
        P("lat", None, None, None, None),
        P("lat", None, None, None, None, None),
        P("krylov", "lat", None, None, None),
    )
    return jax.shard_map(
        shards,
        mesh=mesh,
        in_specs=placed,
        out_specs=(P("lat", None, None, None, None), P("krylov", None, None)),
        check_vma=False,
    )
```

```python
import functools

import jax
import jax.numpy as jnp
from jax import lax
from jax.experimental import pallas as pl
from jax.experimental.pallas import tpu as pltpu
from jax.sharding import PartitionSpec as P

MESH = pl.DeviceIdType.MESH
BF16, F32 = jnp.bfloat16, jnp.float32

DEG = 6
CENTER = 0.25
HALF_WIDTH = 3.25

SITES, NB = 4, 400
QUARTER = 4
ROWS = 2 * QUARTER
FLAT = SITES * 2 * NB
GROUP = 128
CHIPS = 16


def dot(x, w):
    return lax.dot_general(x, w, (((1,), (0,)), ((), ())), preferred_element_type=F32)


def dot_t(x, w):
    return lax.dot_general(x, w, (((1,), (1,)), ((), ())), preferred_element_type=F32)


def turn(x):
    half = x.shape[0] // 2
    if x.shape[0] == ROWS:
        return jnp.concatenate([x[half:], -x[:half]], axis=0)
    return jnp.concatenate(
        [turn(x[i : i + ROWS]) for i in range(0, x.shape[0], ROWS)], axis=0
    )


def kernel(
    start_hbm, self_hbm, hop_hbm, stored_hbm,
    out_ref, coef_ref,
    start, self_w, space_w, time_w, ahead_w, beside_w, stored,
    cur, prev, acc, base, bsend, vrecv, psend, precv,
    asend, arecv, zbuf, dsend, drecv, ssend, srecv, fbuf, ebuf,
    load_sem, vs_sem, vr_sem, ps_sem, pr_sem, gs_sem, gr_sem,
    as_sem, ar_sem, zs_sem, zr_sem, ds_sem, dr_sem, ss_sem, sr_sem,
    fs_sem, fr_sem, es_sem, er_sem, word_sem,
):
    lat, kry = lax.axis_index("lat"), lax.axis_index("krylov")
    y, h = lax.rem(kry, 4), kry // 4
    core, chip = lax.rem(lat, 2), lat // 2
    ahead = (lax.rem(lat + 1, 32), kry)
    behind = (lax.rem(lat + 31, 32), kry)
    partner = (chip * 2 + 1 - core, kry)
    sibling = (lat, (1 - h) * 4 + y)

    def ring(j):
        return lax.rem(y + j, 4)

    def along_y(j):
        return (lat, h * 4 + ring(j))

    def other_chip(j):
        return lax.rem(chip + j, CHIPS)

    barrier = pltpu.get_barrier_semaphore()
    greet = [ahead, behind, sibling]
    greet += [along_y(j) for j in (1, 2, 3)]
    beside_z = [(other_chip(j) * 2 + core, kry) for j in (2, CHIPS - 2)]
    greet += beside_z
    for device in greet:
        pl.semaphore_signal(barrier, inc=1, device_id=device, device_id_type=MESH)

    def remote(src, dst, send_sem, recv_sem, device):
        return pltpu.make_async_remote_copy(
            src_ref=src, dst_ref=dst, send_sem=send_sem, recv_sem=recv_sem,
            device_id=device, device_id_type=MESH,
        )

    loads = [
        pltpu.make_async_copy(hop_hbm.at[:, 1], time_w, load_sem.at[0]),
        pltpu.make_async_copy(self_hbm, self_w, load_sem.at[1]),
        pltpu.make_async_copy(hop_hbm.at[:, 0], space_w, load_sem.at[2]),
        pltpu.make_async_copy(stored_hbm, stored.at[:, pl.ds(0, GROUP)], load_sem.at[3]),
        pltpu.make_async_copy(
            start_hbm.at[:, pl.ds(y * QUARTER, QUARTER)], start, load_sem.at[4]
        ),
    ]
    for q in (4, 0, 1, 2, 3):
        loads[q].start()
    loads[4].wait()
    block = start[...].astype(F32)
    block = jnp.concatenate(
        [block[s, r, c : c + 1] for s in range(SITES) for c in range(2) for r in range(QUARTER)],
        axis=0,
    )
    cur[...] = block
    prev[...] = block
    psend[1] = jnp.zeros_like(psend[1])
    loads[0].wait()

    def flip_time(site, carry):
        ahead_w[site, 0] = jnp.transpose(time_w[site, 0])
        ahead_w[site, 1] = -jnp.transpose(time_w[site, 1])
        return carry

    def flip_space(site, carry):
        beside_w[site, 0] = jnp.transpose(space_w[site, 0])
        beside_w[site, 1] = -jnp.transpose(space_w[site, 1])
        return carry

    lax.fori_loop(0, SITES, flip_time, 0)
    loads[1].wait()
    loads[2].wait()
    lax.fori_loop(0, SITES, flip_space, 0)
    pl.semaphore_wait(barrier, len(greet))

    gathers = [
        remote(
            stored_hbm, stored.at[:, pl.ds(j * GROUP, GROUP)],
            gs_sem.at[j - 1], gr_sem.at[j - 1], along_y(j),
        )
        for j in (1, 2, 3)
    ]

    even, odd = core == 0, core == 1
    halves = (pl.ds(0, 2 * ROWS), pl.ds(2 * ROWS, 2 * ROWS))

    def to_behind(slot, half):
        return remote(
            bsend.at[halves[half]], vrecv.at[slot, halves[half]],
            vs_sem.at[half], vr_sem.at[slot, half], behind,
        )

    def to_ahead(parity, slot, half):
        return remote(
            psend.at[parity, halves[half]], precv.at[slot, halves[half]],
            ps_sem.at[parity, half], pr_sem.at[slot, half], ahead,
        )

    def factor(i):
        first = lax.rem(i, DEG) == 0
        return jnp.where(first, 1.0 / HALF_WIDTH, 2.0 / HALF_WIDTH).astype(F32)

    def meet(i):
        for turn_at in range(5):

            @pl.when(i == 2 * turn_at + 2)
            def _():
                if turn_at > 0:
                    pl.semaphore_wait(word_sem.at[turn_at - 1, 0], 1)
                    pl.semaphore_wait(word_sem.at[turn_at - 1, 1], 1)
                if turn_at < 4:
                    for q, device in enumerate(beside_z):
                        pl.semaphore_signal(
                            word_sem.at[turn_at, q], inc=1, device_id=device, device_id_type=MESH
                        )

    last = 2 * DEG - 1

    def split(half):
        x = cur[halves[half]]
        return [
            (q.astype(BF16), turn(q).astype(BF16)) for q in (x[:ROWS], x[ROWS:])
        ]

    def apply(pair, weight, site):
        return dot(pair[0], weight[site, 0]) + dot(pair[1], weight[site, 1])

    def product(half, i):
        pairs = split(half)
        psend[lax.rem(i, 2), halves[half]] = jnp.concatenate(
            [apply(pairs[q], time_w, 2 * half + q) for q in range(2)], axis=0
        ).astype(BF16)
        to_ahead(lax.rem(i, 2), lax.rem(i, 3), half).start()

    def put(site, value, add=True):
        at = pl.ds(site * ROWS, ROWS)
        acc[at] = acc[at] + value if add else value

    def from_first():
        zero, one = split(0)
        put(0, apply(zero, self_w, 0) + apply(one, beside_w, 0), False)
        put(1, apply(one, self_w, 1) + apply(zero, space_w, 0), False)
        put(2, apply(one, space_w, 1), False)
        put(3, apply(zero, beside_w, 3), False)

    def second_to_first():
        two, three = split(1)
        put(0, apply(three, space_w, 3))
        put(1, apply(two, beside_w, 1))

    def second_to_second():
        two, three = split(1)
        put(2, apply(two, self_w, 2) + apply(three, beside_w, 2))
        put(3, apply(three, self_w, 3) + apply(two, space_w, 2))

    def own_terms(half, i):
        at = halves[half]
        keep = jnp.where(lax.rem(i, DEG) == 0, 0.0, 1.0).astype(F32)
        return factor(i) * (acc[at] - CENTER * cur[at]) - keep * prev[at]

    def from_ahead(half, i, known):
        to_behind(lax.rem(i, 3), half).wait_recv()
        v = vrecv[lax.rem(i, 3), halves[half]].astype(F32)
        if known:
            earlier = lax.rem(i + 1, 2)
            v = v + factor(i + DEG - 1) * psend[earlier, halves[half]].astype(F32)
        pairs = [(q.astype(BF16), turn(q).astype(BF16)) for q in (v[:ROWS], v[ROWS:])]
        return factor(i) * jnp.concatenate(
            [apply(pairs[q], ahead_w, 2 * half + q) for q in range(2)], axis=0
        )

    def finish(half, i, value):
        at = halves[half]
        to_ahead(0, lax.rem(i, 3), half).wait_recv()
        value = value + factor(i) * precv[lax.rem(i, 3), at].astype(F32)
        prev[at] = cur[at]
        cur[at] = value

    def send_behind(half, slot, value):
        to_behind(slot, half).wait_send()
        bsend[halves[half]] = value.astype(BF16)
        to_behind(slot, half).start()

    def next_product(half, i):
        @pl.when(i >= 1)
        def _():
            to_ahead(lax.rem(i + 1, 2), 0, half).wait_send()

        product(half, i + 1)

    def even_step(i):
        second_to_first()
        base[halves[0]] = own_terms(0, i) + from_ahead(0, i, False)

        @pl.when(i < last)
        def _():
            send_behind(0, lax.rem(i + 1, 3), base[halves[0]])

        second_to_second()
        base[halves[1]] = own_terms(1, i) + from_ahead(1, i, False)

        @pl.when(i < last)
        def _():
            send_behind(1, lax.rem(i + 1, 3), base[halves[1]])

        finish(0, i, base[halves[0]])

        @pl.when(i < last)
        def _():
            next_product(0, i)
            from_first()

        finish(1, i, base[halves[1]])

        @pl.when(i < last)
        def _():
            next_product(1, i)

    def odd_step(i):
        from_first()
        second_to_first()
        second_to_second()
        for half in range(2):
            finish(half, i, own_terms(half, i) + from_ahead(half, i, True))

            @pl.when(i < last)
            def _(half=half):
                send_behind(half, lax.rem(i + 1, 3), cur[halves[half]])
                next_product(half, i)

    bsend[...] = cur[...].astype(BF16)
    for half in range(2):
        to_behind(0, half).start()
        product(half, 0)
    for gather in gathers:
        gather.start()

    @pl.when(even)
    def _():
        from_first()

    def step(i, carry):
        meet(i)
        pl.when(even)(lambda: even_step(i))
        pl.when(odd)(lambda: odd_step(i))
        return carry

    lax.fori_loop(0, 2 * DEG, step, 0)
    for half in range(2):
        to_behind(0, half).wait_send()
        to_ahead(0, 0, half).wait_send()
        to_ahead(1, 0, half).wait_send()

    loads[3].wait()
    for gather in gathers:
        gather.wait()

    my_half = pl.ds(pl.multiple_of(core * 2 * GROUP, 2 * GROUP), 2 * GROUP)
    its_half = pl.ds(pl.multiple_of((1 - core) * 2 * GROUP, 2 * GROUP), 2 * GROUP)
    mine_total = other_total = None
    for n in range(2):
        x = cur[...]
        xt = turn(x)
        pieces = []
        for s in range(SITES):
            rows = slice(s * ROWS, s * ROWS + ROWS)
            pieces += [x[rows], xt[rows]]
        pieces = [piece.astype(BF16) for piece in pieces]

        def project(half):
            total = None
            for q, piece in enumerate(pieces):
                term = dot(piece, stored[q * NB : (q + 1) * NB, half])
                total = term if total is None else total + term
            return total

        def spread(coef, half):
            coef = coef.astype(BF16)
            parts = []
            for s in range(SITES):
                at = s * 2 * NB
                real = dot_t(coef, stored[at : at + NB, half])
                imag = dot_t(coef, stored[at + NB : at + 2 * NB, half])
                parts.append(real - turn(imag))
            return jnp.concatenate(parts, axis=0)

        asend[n] = project(its_half)
        cross = remote(asend.at[n], arecv.at[n], as_sem.at[n], ar_sem.at[n], partner)
        cross.start()
        mine = project(my_half)
        cross.wait_recv()
        mine = mine + arecv[n]
        zbuf[n, chip] = jnp.concatenate(
            [mine[:, :GROUP], mine[:, GROUP:]], axis=0
        ).astype(BF16)
        sends = []
        for j in (8, 7, 9, 6, 10, 5, 11, 4, 12, 3, 13, 2, 14, 1, 15):
            sends.append(
                remote(
                    zbuf.at[n, chip], zbuf.at[n, chip], zs_sem.at[n, j], zr_sem.at[n, chip],
                    (other_chip(j) * 2 + core, kry),
                )
            )
        for send in sends:
            send.start()
        for j in range(1, CHIPS):
            source = other_chip(j)
            remote(
                zbuf.at[n, source], zbuf.at[n, source], zs_sem.at[n, j], zr_sem.at[n, source],
                (other_chip(j) * 2 + core, kry),
            ).wait_recv()
        summed = zbuf[n, 0].astype(F32)
        for q in range(1, CHIPS):
            summed = summed + zbuf[n, q].astype(F32)
        own = jnp.concatenate([summed[:ROWS], summed[ROWS:]], axis=1)
        dsend[n] = own
        cross_back = remote(dsend.at[n], drecv.at[n], ds_sem.at[n], dr_sem.at[n], partner)
        cross_back.start()
        change = spread(own, my_half)
        cross_back.wait_recv()
        other = drecv[n]
        mine_total = own if n == 0 else mine_total + own
        other_total = other if n == 0 else other_total + other
        if n == 1:
            low = jnp.where(even, mine_total, other_total)
            high = jnp.where(even, other_total, mine_total)
            ebuf[0, 0], ebuf[0, 1] = low[:, :GROUP], low[:, GROUP:]
            ebuf[0, 2], ebuf[0, 3] = high[:, :GROUP], high[:, GROUP:]
            coef_sends = [
                remote(
                    ebuf.at[0, j], ebuf.at[1, y], es_sem.at[j - 1], er_sem.at[j - 1],
                    along_y(4 - j),
                )
                for j in (1, 2, 3)
            ]
            for send in coef_sends:
                send.start()
        change = change + spread(other, its_half)
        ssend[n] = change.astype(BF16)
        pair = remote(ssend.at[n], srecv.at[n], ss_sem.at[n], sr_sem.at[n], sibling)
        pair.start()
        pair.wait_recv()
        cur[...] = x - (ssend[n].astype(F32) + srecv[n].astype(F32))
        cross.wait_send()
        for send in sends:
            send.wait_send()
        cross_back.wait_send()
        pair.wait_send()

    fbuf[y] = cur[...].astype(BF16)
    final = [
        remote(fbuf.at[y], fbuf.at[y], fs_sem.at[j - 1], fr_sem.at[j - 1], along_y(j))
        for j in (1, 2, 3)
    ]
    for send in final:
        send.start()
    ebuf[1, y] = ebuf[0, 0]
    for j in (1, 2, 3):
        source = ring(j)
        remote(
            ebuf.at[0, j], ebuf.at[1, source], es_sem.at[j - 1], er_sem.at[j - 1], along_y(4 - j)
        ).wait()
    for part in range(2):
        rows = slice(part * QUARTER, (part + 1) * QUARTER)
        coef_ref[part] = jnp.concatenate([ebuf[1, q, rows] for q in range(4)], axis=0)
    for j in (1, 2, 3):
        source = ring(4 - j)
        remote(
            fbuf.at[source], fbuf.at[source], fs_sem.at[j - 1], fr_sem.at[j - 1], along_y(j)
        ).wait_recv()
    for send in final:
        send.wait_send()
    out_ref[...] = fbuf[...]


def shards(start_block, self_block, hop_links, stored_vectors):
    flat = jnp.transpose(stored_vectors.reshape(GROUP, FLAT))
    vmem, anywhere = pltpu.VMEM, pl.BlockSpec(memory_space=pltpu.HBM)
    here = pl.BlockSpec(memory_space=vmem)
    dma, block = pltpu.SemaphoreType.DMA, (SITES * ROWS, NB)
    out, coef = pl.pallas_call(
        kernel,
        out_shape=(
            jax.ShapeDtypeStruct((4,) + block, BF16),
            jax.ShapeDtypeStruct((2, 16, GROUP), F32),
        ),
        in_specs=[anywhere] * 4,
        out_specs=(here, here),
        scratch_shapes=[
            vmem((SITES, QUARTER, 2, NB), BF16),
            vmem((SITES, 2, NB, NB), BF16),
            vmem((SITES, 2, NB, NB), BF16),
            vmem((SITES, 2, NB, NB), BF16),
            vmem((SITES, 2, NB, NB), BF16),
            vmem((SITES, 2, NB, NB), BF16),
            vmem((FLAT, 4 * GROUP), BF16),
            vmem(block, F32),
            vmem(block, F32),
            vmem(block, F32),
            vmem(block, F32),
            vmem(block, BF16),
            vmem((3,) + block, BF16),
            vmem((2,) + block, BF16),
            vmem((3,) + block, BF16),
            vmem((2, ROWS, 2 * GROUP), F32),
            vmem((2, ROWS, 2 * GROUP), F32),
            vmem((2, CHIPS, 2 * ROWS, GROUP), BF16),
            vmem((2, ROWS, 2 * GROUP), F32),
            vmem((2, ROWS, 2 * GROUP), F32),
            vmem((2,) + block, BF16),
            vmem((2,) + block, BF16),
            vmem((4,) + block, BF16),
            vmem((2, 4, ROWS, GROUP), F32),
            dma((5,)),
            dma((2,)), dma((3, 2)), dma((2, 2)), dma((3, 2)),
            dma((3,)), dma((3,)),
            dma((2,)), dma((2,)),
            dma((2, CHIPS)), dma((2, CHIPS)),
            dma((2,)), dma((2,)), dma((2,)), dma((2,)),
            dma((3,)), dma((3,)), dma((3,)), dma((3,)),
            pltpu.SemaphoreType.REGULAR((4, 2)),
        ],
        compiler_params=pltpu.CompilerParams(
            collective_id=0, has_side_effects=True, vmem_limit_bytes=55000 * 2**10
        ),
    )(start_block[0], self_block[0], hop_links[0], flat)
    out = out.reshape(4, SITES, 2, QUARTER, NB)
    out = jnp.transpose(out, (1, 0, 3, 2, 4)).reshape(1, SITES, 16, 2, NB)
    return out, jnp.transpose(coef, (2, 0, 1))


def solution(mesh):
    placed = (
        P("lat", None, None, None, None),
        P("lat", None, None, None, None),
        P("lat", None, None, None, None, None),
        P("krylov", "lat", None, None, None),
    )
    return jax.shard_map(
        shards,
        mesh=mesh,
        in_specs=placed,
        out_specs=(P("lat", None, None, None, None), P("krylov", None, None)),
        check_vma=False,
    )
```

```python
import functools

import jax
import jax.numpy as jnp
from jax import lax
from jax.experimental import pallas as pl
from jax.experimental.pallas import tpu as pltpu
from jax.sharding import PartitionSpec as P

MESH = pl.DeviceIdType.MESH
BF16, F32 = jnp.bfloat16, jnp.float32

DEG = 6
CENTER = 0.25
HALF_WIDTH = 3.25

SITES, NB = 4, 400
QUARTER = 4
ROWS = 2 * QUARTER
FLAT = SITES * 2 * NB
GROUP = 128
CHIPS = 16


def dot(x, w):
    return lax.dot_general(x, w, (((1,), (0,)), ((), ())), preferred_element_type=F32)


def dot_t(x, w):
    return lax.dot_general(x, w, (((1,), (1,)), ((), ())), preferred_element_type=F32)


def turn(x):
    half = x.shape[0] // 2
    if x.shape[0] == ROWS:
        return jnp.concatenate([x[half:], -x[:half]], axis=0)
    return jnp.concatenate(
        [turn(x[i : i + ROWS]) for i in range(0, x.shape[0], ROWS)], axis=0
    )


def kernel(
    start_hbm, self_hbm, hop_hbm, stored_hbm,
    out_ref, coef_ref,
    start, self_w, space_w, time_w, ahead_w, stored,
    cur, prev, acc, base, bsend, vrecv, psend, precv,
    asend, arecv, zbuf, dsend, drecv, ssend, srecv, fbuf, ebuf,
    load_sem, vs_sem, vr_sem, ps_sem, pr_sem, gs_sem, gr_sem,
    as_sem, ar_sem, zs_sem, zr_sem, ds_sem, dr_sem, ss_sem, sr_sem,
    fs_sem, fr_sem, es_sem, er_sem, word_sem,
):
    lat, kry = lax.axis_index("lat"), lax.axis_index("krylov")
    y, h = lax.rem(kry, 4), kry // 4
    core, chip = lax.rem(lat, 2), lat // 2
    ahead = (lax.rem(lat + 1, 32), kry)
    behind = (lax.rem(lat + 31, 32), kry)
    partner = (chip * 2 + 1 - core, kry)
    sibling = (lat, (1 - h) * 4 + y)

    def ring(j):
        return lax.rem(y + j, 4)

    def along_y(j):
        return (lat, h * 4 + ring(j))

    def other_chip(j):
        return lax.rem(chip + j, CHIPS)

    barrier = pltpu.get_barrier_semaphore()
    greet = [ahead, behind, sibling]
    greet += [along_y(j) for j in (1, 2, 3)]
    beside_z = [(other_chip(j) * 2 + core, kry) for j in (2, CHIPS - 2)]
    greet += beside_z
    for device in greet:
        pl.semaphore_signal(barrier, inc=1, device_id=device, device_id_type=MESH)

    def remote(src, dst, send_sem, recv_sem, device):
        return pltpu.make_async_remote_copy(
            src_ref=src, dst_ref=dst, send_sem=send_sem, recv_sem=recv_sem,
            device_id=device, device_id_type=MESH,
        )

    even, odd = core == 0, core == 1
    halves = (pl.ds(0, 2 * ROWS), pl.ds(2 * ROWS, 2 * ROWS))

    def split(half):
        x = cur[halves[half]]
        return [
            (q.astype(BF16), turn(q).astype(BF16)) for q in (x[:ROWS], x[ROWS:])
        ]

    def apply(pair, weight, site):
        return dot(pair[0], weight[site, 0]) + dot(pair[1], weight[site, 1])

    def product(half, i):
        pairs = split(half)
        psend[lax.rem(i, 2), halves[half]] = jnp.concatenate(
            [apply(pairs[q], time_w, 2 * half + q) for q in range(2)], axis=0
        ).astype(BF16)

    def apply_forward(pair, weight, site):
        return dot_t(pair[0], weight[site, 0]) - dot_t(pair[1], weight[site, 1])

    loads = [
        pltpu.make_async_copy(hop_hbm.at[:, 1], time_w, load_sem.at[0]),
        pltpu.make_async_copy(self_hbm, self_w, load_sem.at[1]),
        pltpu.make_async_copy(hop_hbm.at[:, 0], space_w, load_sem.at[2]),
        pltpu.make_async_copy(stored_hbm, stored.at[:, pl.ds(0, GROUP)], load_sem.at[3]),
        pltpu.make_async_copy(
            start_hbm.at[:, pl.ds(y * QUARTER, QUARTER)], start, load_sem.at[4]
        ),
    ]
    for q in (4, 0, 1, 2, 3):
        loads[q].start()
    loads[4].wait()
    block = start[...].astype(F32)
    block = jnp.concatenate(
        [block[s, r, c : c + 1] for s in range(SITES) for c in range(2) for r in range(QUARTER)],
        axis=0,
    )
    cur[...] = block
    prev[...] = block
    psend[1] = jnp.zeros_like(psend[1])
    loads[0].wait()

    for half in range(2):
        product(half, 0)
    for site in range(SITES):
        ahead_w[site, 0] = jnp.transpose(time_w[site, 0])
        ahead_w[site, 1] = -jnp.transpose(time_w[site, 1])
    pl.semaphore_wait(barrier, len(greet))

    gathers = [
        remote(
            stored_hbm, stored.at[:, pl.ds(j * GROUP, GROUP)],
            gs_sem.at[j - 1], gr_sem.at[j - 1], along_y(j),
        )
        for j in (1, 2, 3)
    ]

    def to_behind(slot, half):
        return remote(
            bsend.at[halves[half]], vrecv.at[slot, halves[half]],
            vs_sem.at[half], vr_sem.at[slot, half], behind,
        )

    def to_ahead(parity, slot, half):
        return remote(
            psend.at[parity, halves[half]], precv.at[slot, halves[half]],
            ps_sem.at[parity, half], pr_sem.at[slot, half], ahead,
        )

    def factor(i):
        first = lax.rem(i, DEG) == 0
        return jnp.where(first, 1.0 / HALF_WIDTH, 2.0 / HALF_WIDTH).astype(F32)

    def meet(i):
        for turn_at in range(5):

            @pl.when(i == 2 * turn_at + 2)
            def _():
                if turn_at > 0:
                    pl.semaphore_wait(word_sem.at[turn_at - 1, 0], 1)
                    pl.semaphore_wait(word_sem.at[turn_at - 1, 1], 1)
                if turn_at < 4:
                    for q, device in enumerate(beside_z):
                        pl.semaphore_signal(
                            word_sem.at[turn_at, q], inc=1, device_id=device, device_id_type=MESH
                        )

    last = 2 * DEG - 1

    def put(site, value, add=True):
        at = pl.ds(site * ROWS, ROWS)
        acc[at] = acc[at] + value if add else value

    def from_first():
        zero, one = split(0)
        put(0, apply(zero, self_w, 0) + apply_forward(one, space_w, 0), False)
        put(1, apply(one, self_w, 1) + apply(zero, space_w, 0), False)
        put(2, apply(one, space_w, 1), False)
        put(3, apply_forward(zero, space_w, 3), False)

    def second_to_first():
        two, three = split(1)
        put(0, apply(three, space_w, 3))
        put(1, apply_forward(two, space_w, 1))

    def second_to_second():
        two, three = split(1)
        put(2, apply(two, self_w, 2) + apply_forward(three, space_w, 2))
        put(3, apply(three, self_w, 3) + apply(two, space_w, 2))

    def own_terms(half, i):
        at = halves[half]
        keep = jnp.where(lax.rem(i, DEG) == 0, 0.0, 1.0).astype(F32)
        return factor(i) * (acc[at] - CENTER * cur[at]) - keep * prev[at]

    def from_ahead(half, i, known):
        to_behind(lax.rem(i, 3), half).wait_recv()
        v = vrecv[lax.rem(i, 3), halves[half]].astype(F32)
        if known:
            earlier = lax.rem(i + 1, 2)
            v = v + factor(i + DEG - 1) * psend[earlier, halves[half]].astype(F32)
        pairs = [(q.astype(BF16), turn(q).astype(BF16)) for q in (v[:ROWS], v[ROWS:])]
        return factor(i) * jnp.concatenate(
            [apply(pairs[q], ahead_w, 2 * half + q) for q in range(2)], axis=0
        )

    def finish(half, i, value):
        at = halves[half]
        to_ahead(0, lax.rem(i, 3), half).wait_recv()
        value = value + factor(i) * precv[lax.rem(i, 3), at].astype(F32)
        prev[at] = cur[at]
        cur[at] = value

    def send_behind(half, slot, value):
        to_behind(slot, half).wait_send()
        bsend[halves[half]] = value.astype(BF16)
        to_behind(slot, half).start()

    def next_product(half, i):
        @pl.when(i >= 1)
        def _():
            to_ahead(lax.rem(i + 1, 2), 0, half).wait_send()

        product(half, i + 1)
        to_ahead(lax.rem(i + 1, 2), lax.rem(i + 1, 3), half).start()

    def even_step(i):
        second_to_first()
        base[halves[0]] = own_terms(0, i) + from_ahead(0, i, False)

        @pl.when(i < last)
        def _():
            send_behind(0, lax.rem(i + 1, 3), base[halves[0]])

        second_to_second()
        base[halves[1]] = own_terms(1, i) + from_ahead(1, i, False)

        @pl.when(i < last)
        def _():
            send_behind(1, lax.rem(i + 1, 3), base[halves[1]])

        finish(0, i, base[halves[0]])

        @pl.when(i < last)
        def _():
            next_product(0, i)
            from_first()

        finish(1, i, base[halves[1]])

        @pl.when(i < last)
        def _():
            next_product(1, i)

    def odd_step(i):
        from_first()
        second_to_first()
        second_to_second()
        for half in range(2):
            finish(half, i, own_terms(half, i) + from_ahead(half, i, True))

            @pl.when(i < last)
            def _(half=half):
                send_behind(half, lax.rem(i + 1, 3), cur[halves[half]])
                next_product(half, i)

    bsend[...] = cur[...].astype(BF16)
    for half in range(2):
        to_behind(0, half).start()
        to_ahead(0, 0, half).start()
    for gather in gathers:
        gather.start()
    loads[1].wait()
    loads[2].wait()

    @pl.when(even)
    def _():
        from_first()

    def step(i, carry):
        meet(i)
        pl.when(even)(lambda: even_step(i))
        pl.when(odd)(lambda: odd_step(i))
        return carry

    lax.fori_loop(0, 2 * DEG, step, 0)
    for half in range(2):
        to_behind(0, half).wait_send()
        to_ahead(0, 0, half).wait_send()
        to_ahead(1, 0, half).wait_send()

    loads[3].wait()
    for gather in gathers:
        gather.wait()

    my_half = pl.ds(pl.multiple_of(core * 2 * GROUP, 2 * GROUP), 2 * GROUP)
    its_half = pl.ds(pl.multiple_of((1 - core) * 2 * GROUP, 2 * GROUP), 2 * GROUP)
    mine_total = other_total = None
    for n in range(2):
        x = cur[...]
        xt = turn(x)
        pieces = []
        for s in range(SITES):
            rows = slice(s * ROWS, s * ROWS + ROWS)
            pieces += [x[rows], xt[rows]]
        pieces = [piece.astype(BF16) for piece in pieces]

        def project(half):
            total = None
            for q, piece in enumerate(pieces):
                term = dot(piece, stored[q * NB : (q + 1) * NB, half])
                total = term if total is None else total + term
            return total

        def spread(coef, half):
            coef = coef.astype(BF16)
            parts = []
            for s in range(SITES):
                at = s * 2 * NB
                real = dot_t(coef, stored[at : at + NB, half])
                imag = dot_t(coef, stored[at + NB : at + 2 * NB, half])
                parts.append(real - turn(imag))
            return jnp.concatenate(parts, axis=0)

        asend[n] = project(its_half)
        cross = remote(asend.at[n], arecv.at[n], as_sem.at[n], ar_sem.at[n], partner)
        cross.start()
        mine = project(my_half)
        cross.wait_recv()
        mine = mine + arecv[n]
        zbuf[n, chip] = jnp.concatenate(
            [mine[:, :GROUP], mine[:, GROUP:]], axis=0
        ).astype(BF16)
        sends = []
        for j in (8, 7, 9, 6, 10, 5, 11, 4, 12, 3, 13, 2, 14, 1, 15):
            sends.append(
                remote(
                    zbuf.at[n, chip], zbuf.at[n, chip], zs_sem.at[n, j], zr_sem.at[n, chip],
                    (other_chip(j) * 2 + core, kry),
                )
            )
        for send in sends:
            send.start()
        for j in range(1, CHIPS):
            source = other_chip(j)
            remote(
                zbuf.at[n, source], zbuf.at[n, source], zs_sem.at[n, j], zr_sem.at[n, source],
                (other_chip(j) * 2 + core, kry),
            ).wait_recv()
        summed = zbuf[n, 0].astype(F32)
        for q in range(1, CHIPS):
            summed = summed + zbuf[n, q].astype(F32)
        own = jnp.concatenate([summed[:ROWS], summed[ROWS:]], axis=1)
        dsend[n] = own
        cross_back = remote(dsend.at[n], drecv.at[n], ds_sem.at[n], dr_sem.at[n], partner)
        cross_back.start()
        change = spread(own, my_half)
        cross_back.wait_recv()
        other = drecv[n]
        mine_total = own if n == 0 else mine_total + own
        other_total = other if n == 0 else other_total + other
        if n == 1:
            low = jnp.where(even, mine_total, other_total)
            high = jnp.where(even, other_total, mine_total)
            ebuf[0, 0], ebuf[0, 1] = low[:, :GROUP], low[:, GROUP:]
            ebuf[0, 2], ebuf[0, 3] = high[:, :GROUP], high[:, GROUP:]
            coef_sends = [
                remote(
                    ebuf.at[0, j], ebuf.at[1, y], es_sem.at[j - 1], er_sem.at[j - 1],
                    along_y(4 - j),
                )
                for j in (1, 2, 3)
            ]
            for send in coef_sends:
                send.start()
        change = change + spread(other, its_half)
        ssend[n] = change.astype(BF16)
        pair = remote(ssend.at[n], srecv.at[n], ss_sem.at[n], sr_sem.at[n], sibling)
        pair.start()
        pair.wait_recv()
        cur[...] = x - (ssend[n].astype(F32) + srecv[n].astype(F32))
        cross.wait_send()
        for send in sends:
            send.wait_send()
        cross_back.wait_send()
        pair.wait_send()

    fbuf[y] = cur[...].astype(BF16)
    final = [
        remote(fbuf.at[y], fbuf.at[y], fs_sem.at[j - 1], fr_sem.at[j - 1], along_y(j))
        for j in (1, 2, 3)
    ]
    for send in final:
        send.start()
    ebuf[1, y] = ebuf[0, 0]
    for j in (1, 2, 3):
        source = ring(j)
        remote(
            ebuf.at[0, j], ebuf.at[1, source], es_sem.at[j - 1], er_sem.at[j - 1], along_y(4 - j)
        ).wait()
    for part in range(2):
        rows = slice(part * QUARTER, (part + 1) * QUARTER)
        coef_ref[part] = jnp.concatenate([ebuf[1, q, rows] for q in range(4)], axis=0)
    for j in (1, 2, 3):
        source = ring(4 - j)
        remote(
            fbuf.at[source], fbuf.at[source], fs_sem.at[j - 1], fr_sem.at[j - 1], along_y(j)
        ).wait_recv()
    for send in final:
        send.wait_send()
    out_ref[...] = fbuf[...]


def shards(start_block, self_block, hop_links, stored_vectors):
    flat = jnp.transpose(stored_vectors.reshape(GROUP, FLAT))
    vmem, anywhere = pltpu.VMEM, pl.BlockSpec(memory_space=pltpu.HBM)
    here = pl.BlockSpec(memory_space=vmem)
    dma, block = pltpu.SemaphoreType.DMA, (SITES * ROWS, NB)
    out, coef = pl.pallas_call(
        kernel,
        out_shape=(
            jax.ShapeDtypeStruct((4,) + block, BF16),
            jax.ShapeDtypeStruct((2, 16, GROUP), F32),
        ),
        in_specs=[anywhere] * 4,
        out_specs=(here, here),
        scratch_shapes=[
            vmem((SITES, QUARTER, 2, NB), BF16),
            vmem((SITES, 2, NB, NB), BF16),
            vmem((SITES, 2, NB, NB), BF16),
            vmem((SITES, 2, NB, NB), BF16),
            vmem((SITES, 2, NB, NB), BF16),
            vmem((FLAT, 4 * GROUP), BF16),
            vmem(block, F32),
            vmem(block, F32),
            vmem(block, F32),
            vmem(block, F32),
            vmem(block, BF16),
            vmem((3,) + block, BF16),
            vmem((2,) + block, BF16),
            vmem((3,) + block, BF16),
            vmem((2, ROWS, 2 * GROUP), F32),
            vmem((2, ROWS, 2 * GROUP), F32),
            vmem((2, CHIPS, 2 * ROWS, GROUP), BF16),
            vmem((2, ROWS, 2 * GROUP), F32),
            vmem((2, ROWS, 2 * GROUP), F32),
            vmem((2,) + block, BF16),
            vmem((2,) + block, BF16),
            vmem((4,) + block, BF16),
            vmem((2, 4, ROWS, GROUP), F32),
            dma((5,)),
            dma((2,)), dma((3, 2)), dma((2, 2)), dma((3, 2)),
            dma((3,)), dma((3,)),
            dma((2,)), dma((2,)),
            dma((2, CHIPS)), dma((2, CHIPS)),
            dma((2,)), dma((2,)), dma((2,)), dma((2,)),
            dma((3,)), dma((3,)), dma((3,)), dma((3,)),
            pltpu.SemaphoreType.REGULAR((4, 2)),
        ],
        compiler_params=pltpu.CompilerParams(
            collective_id=0, has_side_effects=True, vmem_limit_bytes=55000 * 2**10
        ),
    )(start_block[0], self_block[0], hop_links[0], flat)
    out = out.reshape(4, SITES, 2, QUARTER, NB)
    out = jnp.transpose(out, (1, 0, 3, 2, 4)).reshape(1, SITES, 16, 2, NB)
    return out, jnp.transpose(coef, (2, 0, 1))


def solution(mesh):
    placed = (
        P("lat", None, None, None, None),
        P("lat", None, None, None, None),
        P("lat", None, None, None, None, None),
        P("krylov", "lat", None, None, None),
    )
    return jax.shard_map(
        shards,
        mesh=mesh,
        in_specs=placed,
        out_specs=(P("lat", None, None, None, None), P("krylov", None, None)),
        check_vma=False,
    )
```

```python
import functools

import jax
import jax.numpy as jnp
from jax import lax
from jax.experimental import pallas as pl
from jax.experimental.pallas import tpu as pltpu
from jax.sharding import PartitionSpec as P

MESH = pl.DeviceIdType.MESH
BF16, F32 = jnp.bfloat16, jnp.float32

DEG = 6
CENTER = 0.25
HALF_WIDTH = 3.25

SITES, NB = 4, 400
QUARTER = 4
ROWS = 2 * QUARTER
FLAT = SITES * 2 * NB
GROUP = 128
CHIPS = 16


def dot(x, w):
    return lax.dot_general(x, w, (((1,), (0,)), ((), ())), preferred_element_type=F32)


def dot_t(x, w):
    return lax.dot_general(x, w, (((1,), (1,)), ((), ())), preferred_element_type=F32)


def turn(x):
    half = x.shape[0] // 2
    if x.shape[0] == ROWS:
        return jnp.concatenate([x[half:], -x[:half]], axis=0)
    return jnp.concatenate(
        [turn(x[i : i + ROWS]) for i in range(0, x.shape[0], ROWS)], axis=0
    )


def kernel(
    start_hbm, self_hbm, hop_hbm, stored_hbm,
    out_ref, coef_ref,
    start, self_w, space_w, time_w, ahead_w, beside_w, stored,
    cur, prev, acc, base, bsend, vrecv, psend, precv,
    asend, arecv, zbuf, dsend, drecv, ssend, srecv, fbuf, ebuf,
    load_sem, vs_sem, vr_sem, ps_sem, pr_sem, gs_sem, gr_sem,
    as_sem, ar_sem, zs_sem, zr_sem, ds_sem, dr_sem, ss_sem, sr_sem,
    fs_sem, fr_sem, es_sem, er_sem, word_sem,
):
    lat, kry = lax.axis_index("lat"), lax.axis_index("krylov")
    y, h = lax.rem(kry, 4), kry // 4
    core, chip = lax.rem(lat, 2), lat // 2
    ahead = (lax.rem(lat + 1, 32), kry)
    behind = (lax.rem(lat + 31, 32), kry)
    partner = (chip * 2 + 1 - core, kry)
    sibling = (lat, (1 - h) * 4 + y)

    def ring(j):
        return lax.rem(y + j, 4)

    def along_y(j):
        return (lat, h * 4 + ring(j))

    def other_chip(j):
        return lax.rem(chip + j, CHIPS)

    barrier = pltpu.get_barrier_semaphore()
    greet = [ahead, behind, sibling]
    greet += [along_y(j) for j in (1, 2, 3)]
    beside_z = [(other_chip(j) * 2 + core, kry) for j in (2, CHIPS - 2)]
    greet += beside_z
    for device in greet:
        pl.semaphore_signal(barrier, inc=1, device_id=device, device_id_type=MESH)

    def remote(src, dst, send_sem, recv_sem, device):
        return pltpu.make_async_remote_copy(
            src_ref=src, dst_ref=dst, send_sem=send_sem, recv_sem=recv_sem,
            device_id=device, device_id_type=MESH,
        )

    even, odd = core == 0, core == 1
    halves = (pl.ds(0, 2 * ROWS), pl.ds(2 * ROWS, 2 * ROWS))

    def split(half):
        x = cur[halves[half]]
        return [
            (q.astype(BF16), turn(q).astype(BF16)) for q in (x[:ROWS], x[ROWS:])
        ]

    def apply(pair, weight, site):
        return dot(pair[0], weight[site, 0]) + dot(pair[1], weight[site, 1])

    def product(half, i):
        pairs = split(half)
        psend[lax.rem(i, 2), halves[half]] = jnp.concatenate(
            [apply(pairs[q], time_w, 2 * half + q) for q in range(2)], axis=0
        ).astype(BF16)

    loads = [
        pltpu.make_async_copy(hop_hbm.at[:, 1], time_w, load_sem.at[0]),
        pltpu.make_async_copy(self_hbm, self_w, load_sem.at[1]),
        pltpu.make_async_copy(hop_hbm.at[:, 0], space_w, load_sem.at[2]),
        pltpu.make_async_copy(stored_hbm, stored.at[:, pl.ds(0, GROUP)], load_sem.at[3]),
        pltpu.make_async_copy(
            start_hbm.at[:, pl.ds(y * QUARTER, QUARTER)], start, load_sem.at[4]
        ),
    ]
    for q in (4, 0, 2, 1, 3):
        loads[q].start()
    loads[4].wait()
    block = start[...].astype(F32)
    block = jnp.concatenate(
        [block[s, r, c : c + 1] for s in range(SITES) for c in range(2) for r in range(QUARTER)],
        axis=0,
    )
    cur[...] = block
    prev[...] = block
    psend[1] = jnp.zeros_like(psend[1])
    loads[0].wait()

    for half in range(2):
        product(half, 0)

    def unit(n):
        row = lax.broadcasted_iota(jnp.int32, (n, n), 0)
        return (row == lax.broadcasted_iota(jnp.int32, (n, n), 1)).astype(BF16)

    def flip(weight, flipped, by_product):
        for site in range(SITES):
            for part in range(2):
                source = weight[site, part]
                if (site, part) in by_product:
                    value = jnp.concatenate(
                        [dot_t(unit(256), source[:, :256]), dot_t(unit(144), source[:, 256:])], axis=0
                    ).astype(BF16)
                else:
                    value = jnp.transpose(source)
                flipped[site, part] = -value if part else value

    flip(time_w, ahead_w, ((1, 0), (3, 0)))
    loads[2].wait()
    flip(space_w, beside_w, ((0, 1), (1, 1), (2, 1)))
    pl.semaphore_wait(barrier, len(greet))

    gathers = [
        remote(
            stored_hbm, stored.at[:, pl.ds(j * GROUP, GROUP)],
            gs_sem.at[j - 1], gr_sem.at[j - 1], along_y(j),
        )
        for j in (1, 2, 3)
    ]

    def to_behind(slot, half):
        return remote(
            bsend.at[halves[half]], vrecv.at[slot, halves[half]],
            vs_sem.at[half], vr_sem.at[slot, half], behind,
        )

    def to_ahead(parity, slot, half):
        return remote(
            psend.at[parity, halves[half]], precv.at[slot, halves[half]],
            ps_sem.at[parity, half], pr_sem.at[slot, half], ahead,
        )

    def factor(i):
        first = lax.rem(i, DEG) == 0
        return jnp.where(first, 1.0 / HALF_WIDTH, 2.0 / HALF_WIDTH).astype(F32)

    def meet(i):
        for turn_at in range(5):

            @pl.when(i == 2 * turn_at + 2)
            def _():
                if turn_at > 0:
                    pl.semaphore_wait(word_sem.at[turn_at - 1, 0], 1)
                    pl.semaphore_wait(word_sem.at[turn_at - 1, 1], 1)
                if turn_at < 4:
                    for q, device in enumerate(beside_z):
                        pl.semaphore_signal(
                            word_sem.at[turn_at, q], inc=1, device_id=device, device_id_type=MESH
                        )

    last = 2 * DEG - 1

    def put(site, value, add=True):
        at = pl.ds(site * ROWS, ROWS)
        acc[at] = acc[at] + value if add else value

    def from_first():
        zero, one = split(0)
        put(0, apply(zero, self_w, 0) + apply(one, beside_w, 0), False)
        put(1, apply(one, self_w, 1) + apply(zero, space_w, 0), False)
        put(2, apply(one, space_w, 1), False)
        put(3, apply(zero, beside_w, 3), False)

    def second_to_first():
        two, three = split(1)
        put(0, apply(three, space_w, 3))
        put(1, apply(two, beside_w, 1))

    def second_to_second():
        two, three = split(1)
        put(2, apply(two, self_w, 2) + apply(three, beside_w, 2))
        put(3, apply(three, self_w, 3) + apply(two, space_w, 2))

    def own_terms(half, i):
        at = halves[half]
        keep = jnp.where(lax.rem(i, DEG) == 0, 0.0, 1.0).astype(F32)
        return factor(i) * (acc[at] - CENTER * cur[at]) - keep * prev[at]

    def from_ahead(half, i, known):
        to_behind(lax.rem(i, 3), half).wait_recv()
        v = vrecv[lax.rem(i, 3), halves[half]].astype(F32)
        if known:
            earlier = lax.rem(i + 1, 2)
            v = v + factor(i + DEG - 1) * psend[earlier, halves[half]].astype(F32)
        pairs = [(q.astype(BF16), turn(q).astype(BF16)) for q in (v[:ROWS], v[ROWS:])]
        return factor(i) * jnp.concatenate(
            [apply(pairs[q], ahead_w, 2 * half + q) for q in range(2)], axis=0
        )

    def finish(half, i, value):
        at = halves[half]
        to_ahead(0, lax.rem(i, 3), half).wait_recv()
        value = value + factor(i) * precv[lax.rem(i, 3), at].astype(F32)
        prev[at] = cur[at]
        cur[at] = value

    def send_behind(half, slot, value):
        to_behind(slot, half).wait_send()
        bsend[halves[half]] = value.astype(BF16)
        to_behind(slot, half).start()

    def next_product(half, i):
        @pl.when(i >= 1)
        def _():
            to_ahead(lax.rem(i + 1, 2), 0, half).wait_send()

        product(half, i + 1)
        to_ahead(lax.rem(i + 1, 2), lax.rem(i + 1, 3), half).start()

    def even_step(i):
        second_to_first()
        base[halves[0]] = own_terms(0, i) + from_ahead(0, i, False)

        @pl.when(i < last)
        def _():
            send_behind(0, lax.rem(i + 1, 3), base[halves[0]])

        second_to_second()
        base[halves[1]] = own_terms(1, i) + from_ahead(1, i, False)

        @pl.when(i < last)
        def _():
            send_behind(1, lax.rem(i + 1, 3), base[halves[1]])

        finish(0, i, base[halves[0]])

        @pl.when(i < last)
        def _():
            next_product(0, i)
            from_first()

        finish(1, i, base[halves[1]])

        @pl.when(i < last)
        def _():
            next_product(1, i)

    def odd_step(i):
        from_first()
        second_to_first()
        second_to_second()
        for half in range(2):
            finish(half, i, own_terms(half, i) + from_ahead(half, i, True))

            @pl.when(i < last)
            def _(half=half):
                send_behind(half, lax.rem(i + 1, 3), cur[halves[half]])
                next_product(half, i)

    bsend[...] = cur[...].astype(BF16)
    for half in range(2):
        to_behind(0, half).start()
        to_ahead(0, 0, half).start()
    for gather in gathers:
        gather.start()
    loads[1].wait()

    @pl.when(even)
    def _():
        from_first()

    def step(i, carry):
        meet(i)
        pl.when(even)(lambda: even_step(i))
        pl.when(odd)(lambda: odd_step(i))
        return carry

    lax.fori_loop(0, 2 * DEG, step, 0)
    for half in range(2):
        to_behind(0, half).wait_send()
        to_ahead(0, 0, half).wait_send()
        to_ahead(1, 0, half).wait_send()

    loads[3].wait()
    for gather in gathers:
        gather.wait()

    my_half = pl.ds(pl.multiple_of(core * 2 * GROUP, 2 * GROUP), 2 * GROUP)
    its_half = pl.ds(pl.multiple_of((1 - core) * 2 * GROUP, 2 * GROUP), 2 * GROUP)
    mine_total = other_total = None

    def project(half, columns):
        total = None
        for q, pair in enumerate(split(half)):
            for part in range(2):
                at = ((2 * half + q) * 2 + part) * NB
                term = dot(pair[part], stored[at : at + NB, columns])
                total = term if total is None else total + term
        return total

    def spread(coef, half, columns):
        coef = coef.astype(BF16)
        parts = []
        for site in (2 * half, 2 * half + 1):
            at = site * 2 * NB
            real = dot_t(coef, stored[at : at + NB, columns])
            imag = dot_t(coef, stored[at + NB : at + 2 * NB, columns])
            parts.append(real - turn(imag))
        return jnp.concatenate(parts, axis=0)

    final = []
    theirs = project(0, its_half) + project(1, its_half)
    for n in range(2):
        asend[n] = theirs
        cross = remote(asend.at[n], arecv.at[n], as_sem.at[n], ar_sem.at[n], partner)
        cross.start()
        mine = project(0, my_half) + project(1, my_half)
        cross.wait_recv()
        mine = mine + arecv[n]
        zbuf[n, chip] = jnp.concatenate(
            [mine[:, :GROUP], mine[:, GROUP:]], axis=0
        ).astype(BF16)
        sends = []
        for j in (8, 7, 9, 6, 10, 5, 11, 4, 12, 3, 13, 2, 14, 1, 15):
            sends.append(
                remote(
                    zbuf.at[n, chip], zbuf.at[n, chip], zs_sem.at[n, j], zr_sem.at[n, chip],
                    (other_chip(j) * 2 + core, kry),
                )
            )
        for send in sends:
            send.start()
        for j in range(1, CHIPS):
            source = other_chip(j)
            remote(
                zbuf.at[n, source], zbuf.at[n, source], zs_sem.at[n, j], zr_sem.at[n, source],
                (other_chip(j) * 2 + core, kry),
            ).wait_recv()
        summed = zbuf[n, 0].astype(F32)
        for q in range(1, CHIPS):
            summed = summed + zbuf[n, q].astype(F32)
        own = jnp.concatenate([summed[:ROWS], summed[ROWS:]], axis=1)
        dsend[n] = own
        cross_back = remote(dsend.at[n], drecv.at[n], ds_sem.at[n], dr_sem.at[n], partner)
        cross_back.start()
        change = [spread(own, half, my_half) for half in range(2)]
        cross_back.wait_recv()
        other = drecv[n]
        mine_total = own if n == 0 else mine_total + own
        other_total = other if n == 0 else other_total + other
        if n == 1:
            low = jnp.where(even, mine_total, other_total)
            high = jnp.where(even, other_total, mine_total)
            ebuf[0, 0], ebuf[0, 1] = low[:, :GROUP], low[:, GROUP:]
            ebuf[0, 2], ebuf[0, 3] = high[:, :GROUP], high[:, GROUP:]
            coef_sends = [
                remote(
                    ebuf.at[0, j], ebuf.at[1, y], es_sem.at[j - 1], er_sem.at[j - 1],
                    along_y(4 - j),
                )
                for j in (1, 2, 3)
            ]
            for send in coef_sends:
                send.start()
        pairs = []
        for half in range(2):
            at = halves[half]
            ssend[n, at] = (change[half] + spread(other, half, its_half)).astype(BF16)
            pair = remote(
                ssend.at[n, at], srecv.at[n, at], ss_sem.at[n, half], sr_sem.at[n, half], sibling
            )
            pair.start()
            pairs.append(pair)
        for half in range(2):
            at = halves[half]
            pairs[half].wait_recv()
            cur[at] = cur[at] - (ssend[n, at].astype(F32) + srecv[n, at].astype(F32))
            if n == 0:
                term = project(half, its_half)
                theirs = term if half == 0 else theirs + term
            else:
                fbuf[y, at] = cur[at].astype(BF16)
                for j in (2, 1, 3):
                    send = remote(
                        fbuf.at[y, at], fbuf.at[y, at],
                        fs_sem.at[j - 1, half], fr_sem.at[j - 1, half], along_y(j),
                    )
                    send.start()
                    final.append(send)
        cross.wait_send()
        for send in sends:
            send.wait_send()
        cross_back.wait_send()
        for pair in pairs:
            pair.wait_send()

    ebuf[1, y] = ebuf[0, 0]
    for j in (1, 2, 3):
        source = ring(j)
        remote(
            ebuf.at[0, j], ebuf.at[1, source], es_sem.at[j - 1], er_sem.at[j - 1], along_y(4 - j)
        ).wait()
    for part in range(2):
        rows = slice(part * QUARTER, (part + 1) * QUARTER)
        coef_ref[part] = jnp.concatenate([ebuf[1, q, rows] for q in range(4)], axis=0)
    for j in (1, 2, 3):
        source = ring(4 - j)
        for half in range(2):
            at = halves[half]
            remote(
                fbuf.at[source, at], fbuf.at[source, at],
                fs_sem.at[j - 1, half], fr_sem.at[j - 1, half], along_y(j),
            ).wait_recv()
    for send in final:
        send.wait_send()
    out_ref[...] = fbuf[...]


def shards(start_block, self_block, hop_links, stored_vectors):
    flat = jnp.transpose(stored_vectors.reshape(GROUP, FLAT))
    vmem, anywhere = pltpu.VMEM, pl.BlockSpec(memory_space=pltpu.HBM)
    here = pl.BlockSpec(memory_space=vmem)
    dma, block = pltpu.SemaphoreType.DMA, (SITES * ROWS, NB)
    out, coef = pl.pallas_call(
        kernel,
        out_shape=(
            jax.ShapeDtypeStruct((4,) + block, BF16),
            jax.ShapeDtypeStruct((2, 16, GROUP), F32),
        ),
        in_specs=[anywhere] * 4,
        out_specs=(here, here),
        scratch_shapes=[
            vmem((SITES, QUARTER, 2, NB), BF16),
            vmem((SITES, 2, NB, NB), BF16),
            vmem((SITES, 2, NB, NB), BF16),
            vmem((SITES, 2, NB, NB), BF16),
            vmem((SITES, 2, NB, NB), BF16),
            vmem((SITES, 2, NB, NB), BF16),
            vmem((FLAT, 4 * GROUP), BF16),
            vmem(block, F32),
            vmem(block, F32),
            vmem(block, F32),
            vmem(block, F32),
            vmem(block, BF16),
            vmem((3,) + block, BF16),
            vmem((2,) + block, BF16),
            vmem((3,) + block, BF16),
            vmem((2, ROWS, 2 * GROUP), F32),
            vmem((2, ROWS, 2 * GROUP), F32),
            vmem((2, CHIPS, 2 * ROWS, GROUP), BF16),
            vmem((2, ROWS, 2 * GROUP), F32),
            vmem((2, ROWS, 2 * GROUP), F32),
            vmem((2,) + block, BF16),
            vmem((2,) + block, BF16),
            vmem((4,) + block, BF16),
            vmem((2, 4, ROWS, GROUP), F32),
            dma((5,)),
            dma((2,)), dma((3, 2)), dma((2, 2)), dma((3, 2)),
            dma((3,)), dma((3,)),
            dma((2,)), dma((2,)),
            dma((2, CHIPS)), dma((2, CHIPS)),
            dma((2,)), dma((2,)), dma((2, 2)), dma((2, 2)),
            dma((3, 2)), dma((3, 2)), dma((3,)), dma((3,)),
            pltpu.SemaphoreType.REGULAR((4, 2)),
        ],
        compiler_params=pltpu.CompilerParams(
            collective_id=0, has_side_effects=True, vmem_limit_bytes=55000 * 2**10
        ),
    )(start_block[0], self_block[0], hop_links[0], flat)
    out = out.reshape(4, SITES, 2, QUARTER, NB)
    out = jnp.transpose(out, (1, 0, 3, 2, 4)).reshape(1, SITES, 16, 2, NB)
    return out, jnp.transpose(coef, (2, 0, 1))


def solution(mesh):
    placed = (
        P("lat", None, None, None, None),
        P("lat", None, None, None, None),
        P("lat", None, None, None, None, None),
        P("krylov", "lat", None, None, None),
    )
    return jax.shard_map(
        shards,
        mesh=mesh,
        in_specs=placed,
        out_specs=(P("lat", None, None, None, None), P("krylov", None, None)),
        check_vma=False,
    )
```

```python
import functools

import jax
import jax.numpy as jnp
from jax import lax
from jax.experimental import pallas as pl
from jax.experimental.pallas import tpu as pltpu
from jax.sharding import PartitionSpec as P

MESH = pl.DeviceIdType.MESH
BF16, F32 = jnp.bfloat16, jnp.float32

DEG = 6
CENTER = 0.25
HALF_WIDTH = 3.25

SITES, NB = 4, 400
QUARTER = 4
ROWS = 2 * QUARTER
FLAT = SITES * 2 * NB
GROUP = 128
CHIPS = 16


def dot(x, w):
    return lax.dot_general(x, w, (((1,), (0,)), ((), ())), preferred_element_type=F32)


def dot_t(x, w):
    return lax.dot_general(x, w, (((1,), (1,)), ((), ())), preferred_element_type=F32)


def turn(x):
    half = x.shape[0] // 2
    if x.shape[0] == ROWS:
        return jnp.concatenate([x[half:], -x[:half]], axis=0)
    return jnp.concatenate(
        [turn(x[i : i + ROWS]) for i in range(0, x.shape[0], ROWS)], axis=0
    )


def kernel(
    start_hbm, self_hbm, hop_hbm, stored_hbm,
    out_ref, coef_ref,
    start, self_w, space_w, time_w, ahead_w, beside_w, stored,
    cur, prev, acc, base, bsend, vrecv, psend, precv,
    asend, arecv, zbuf, dsend, drecv, ssend, srecv, fbuf, ebuf,
    load_sem, vs_sem, vr_sem, ps_sem, pr_sem, gs_sem, gr_sem,
    as_sem, ar_sem, zs_sem, zr_sem, ds_sem, dr_sem, ss_sem, sr_sem,
    fs_sem, fr_sem, es_sem, er_sem, word_sem,
):
    lat, kry = lax.axis_index("lat"), lax.axis_index("krylov")
    y, h = lax.rem(kry, 4), kry // 4
    core, chip = lax.rem(lat, 2), lat // 2
    ahead = (lax.rem(lat + 1, 32), kry)
    behind = (lax.rem(lat + 31, 32), kry)
    partner = (chip * 2 + 1 - core, kry)
    sibling = (lat, (1 - h) * 4 + y)

    def ring(j):
        return lax.rem(y + j, 4)

    def along_y(j):
        return (lat, h * 4 + ring(j))

    def other_chip(j):
        return lax.rem(chip + j, CHIPS)

    barrier = pltpu.get_barrier_semaphore()
    greet = [ahead, behind, sibling]
    greet += [along_y(j) for j in (1, 2, 3)]
    beside_z = [(other_chip(j) * 2 + core, kry) for j in (2, CHIPS - 2)]
    greet += beside_z
    for device in greet:
        pl.semaphore_signal(barrier, inc=1, device_id=device, device_id_type=MESH)

    def remote(src, dst, send_sem, recv_sem, device):
        return pltpu.make_async_remote_copy(
            src_ref=src, dst_ref=dst, send_sem=send_sem, recv_sem=recv_sem,
            device_id=device, device_id_type=MESH,
        )

    even, odd = core == 0, core == 1
    halves = (pl.ds(0, 2 * ROWS), pl.ds(2 * ROWS, 2 * ROWS))

    def split(half):
        x = cur[halves[half]]
        return [
            (q.astype(BF16), turn(q).astype(BF16)) for q in (x[:ROWS], x[ROWS:])
        ]

    def apply(pair, weight, site):
        return dot(pair[0], weight[site, 0]) + dot(pair[1], weight[site, 1])

    def product(half, i):
        pairs = split(half)
        psend[lax.rem(i, 2), halves[half]] = jnp.concatenate(
            [apply(pairs[q], time_w, 2 * half + q) for q in range(2)], axis=0
        ).astype(BF16)

    first_load = pltpu.make_async_copy(
        start_hbm.at[:, pl.ds(y * QUARTER, QUARTER)], start, load_sem.at[3 * SITES]
    )
    last_load = pltpu.make_async_copy(
        stored_hbm, stored.at[:, pl.ds(0, GROUP)], load_sem.at[3 * SITES + 1]
    )
    time_loads = [
        pltpu.make_async_copy(hop_hbm.at[q, 1], time_w.at[q], load_sem.at[q])
        for q in range(SITES)
    ]
    space_loads = [
        pltpu.make_async_copy(hop_hbm.at[q, 0], space_w.at[q], load_sem.at[SITES + q])
        for q in range(SITES)
    ]
    self_loads = [
        pltpu.make_async_copy(self_hbm.at[q], self_w.at[q], load_sem.at[2 * SITES + q])
        for q in range(SITES)
    ]
    for load in [first_load] + time_loads + space_loads + self_loads + [last_load]:
        load.start()
    first_load.wait()
    block = start[...].astype(F32)
    block = jnp.concatenate(
        [block[s, r, c : c + 1] for s in range(SITES) for c in range(2) for r in range(QUARTER)],
        axis=0,
    )
    cur[...] = block
    prev[...] = block
    psend[1] = jnp.zeros_like(psend[1])
    def unit(n):
        row = lax.broadcasted_iota(jnp.int32, (n, n), 0)
        return (row == lax.broadcasted_iota(jnp.int32, (n, n), 1)).astype(BF16)

    def flip(weight, flipped, site):
        source = weight[site, 0]
        flipped[site, 0] = jnp.concatenate(
            [dot_t(unit(256), source[:, :256]), dot_t(unit(144), source[:, 256:])], axis=0
        ).astype(BF16)
        flipped[site, 1] = -jnp.transpose(weight[site, 1])

    for site in range(SITES):
        time_loads[site].wait()
        if site % 2:
            product(site // 2, 0)
        flip(time_w, ahead_w, site)
    pl.semaphore_wait(barrier, len(greet))

    gathers = [
        remote(
            stored_hbm, stored.at[:, pl.ds(j * GROUP, GROUP)],
            gs_sem.at[j - 1], gr_sem.at[j - 1], along_y(j),
        )
        for j in (1, 2, 3)
    ]

    def to_behind(slot, half):
        return remote(
            bsend.at[halves[half]], vrecv.at[slot, halves[half]],
            vs_sem.at[half], vr_sem.at[slot, half], behind,
        )

    def to_ahead(parity, slot, half):
        return remote(
            psend.at[parity, halves[half]], precv.at[slot, halves[half]],
            ps_sem.at[parity, half], pr_sem.at[slot, half], ahead,
        )

    def factor(i):
        first = lax.rem(i, DEG) == 0
        return jnp.where(first, 1.0 / HALF_WIDTH, 2.0 / HALF_WIDTH).astype(F32)

    def meet(i):
        for turn_at in range(5):

            @pl.when(i == 2 * turn_at + 2)
            def _():
                if turn_at > 0:
                    pl.semaphore_wait(word_sem.at[turn_at - 1, 0], 1)
                    pl.semaphore_wait(word_sem.at[turn_at - 1, 1], 1)
                if turn_at < 4:
                    for q, device in enumerate(beside_z):
                        pl.semaphore_signal(
                            word_sem.at[turn_at, q], inc=1, device_id=device, device_id_type=MESH
                        )

    last = 2 * DEG - 1

    def put(site, value, add=True):
        at = pl.ds(site * ROWS, ROWS)
        acc[at] = acc[at] + value if add else value

    def from_first():
        zero, one = split(0)
        put(0, apply(zero, self_w, 0) + apply(one, beside_w, 0), False)
        put(1, apply(one, self_w, 1) + apply(zero, space_w, 0), False)
        put(2, apply(one, space_w, 1), False)
        put(3, apply(zero, beside_w, 3), False)

    def second_to_first():
        two, three = split(1)
        put(0, apply(three, space_w, 3))
        put(1, apply(two, beside_w, 1))

    def second_to_second():
        two, three = split(1)
        put(2, apply(two, self_w, 2) + apply(three, beside_w, 2))
        put(3, apply(three, self_w, 3) + apply(two, space_w, 2))

    def own_terms(half, i):
        at = halves[half]
        keep = jnp.where(lax.rem(i, DEG) == 0, 0.0, 1.0).astype(F32)
        return factor(i) * (acc[at] - CENTER * cur[at]) - keep * prev[at]

    def from_ahead(half, i, known):
        to_behind(lax.rem(i, 3), half).wait_recv()
        v = vrecv[lax.rem(i, 3), halves[half]].astype(F32)
        if known:
            earlier = lax.rem(i + 1, 2)
            v = v + factor(i + DEG - 1) * psend[earlier, halves[half]].astype(F32)
        pairs = [(q.astype(BF16), turn(q).astype(BF16)) for q in (v[:ROWS], v[ROWS:])]
        return factor(i) * jnp.concatenate(
            [apply(pairs[q], ahead_w, 2 * half + q) for q in range(2)], axis=0
        )

    def finish(half, i, value):
        at = halves[half]
        to_ahead(0, lax.rem(i, 3), half).wait_recv()
        value = value + factor(i) * precv[lax.rem(i, 3), at].astype(F32)
        prev[at] = cur[at]
        cur[at] = value

    def send_behind(half, slot, value):
        to_behind(slot, half).wait_send()
        bsend[halves[half]] = value.astype(BF16)
        to_behind(slot, half).start()

    def next_product(half, i):
        @pl.when(i >= 1)
        def _():
            to_ahead(lax.rem(i + 1, 2), 0, half).wait_send()

        product(half, i + 1)
        to_ahead(lax.rem(i + 1, 2), lax.rem(i + 1, 3), half).start()

    def even_step(i):
        second_to_first()
        base[halves[0]] = own_terms(0, i) + from_ahead(0, i, False)

        @pl.when(i < last)
        def _():
            send_behind(0, lax.rem(i + 1, 3), base[halves[0]])

        second_to_second()
        base[halves[1]] = own_terms(1, i) + from_ahead(1, i, False)

        @pl.when(i < last)
        def _():
            send_behind(1, lax.rem(i + 1, 3), base[halves[1]])

        finish(0, i, base[halves[0]])

        @pl.when(i < last)
        def _():
            next_product(0, i)
            from_first()

        finish(1, i, base[halves[1]])

        @pl.when(i < last)
        def _():
            next_product(1, i)

    def odd_step(i):
        from_first()
        second_to_first()
        second_to_second()
        for half in range(2):
            finish(half, i, own_terms(half, i) + from_ahead(half, i, True))

            @pl.when(i < last)
            def _(half=half):
                next_product(half, i)
                send_behind(half, lax.rem(i + 1, 3), cur[halves[half]])

    bsend[...] = cur[...].astype(BF16)
    for half in range(2):
        to_behind(0, half).start()
        to_ahead(0, 0, half).start()
    for gather in gathers:
        gather.start()
    for site in range(SITES):
        space_loads[site].wait()
        flip(space_w, beside_w, site)
    for load in self_loads:
        load.wait()

    @pl.when(even)
    def _():
        from_first()

    def step(i, carry):
        meet(i)
        pl.when(even)(lambda: even_step(i))
        pl.when(odd)(lambda: odd_step(i))
        return carry

    lax.fori_loop(0, 2 * DEG, step, 0)
    for half in range(2):
        to_behind(0, half).wait_send()
        to_ahead(0, 0, half).wait_send()
        to_ahead(1, 0, half).wait_send()

    last_load.wait()
    for gather in gathers:
        gather.wait()

    my_half = pl.ds(pl.multiple_of(core * 2 * GROUP, 2 * GROUP), 2 * GROUP)
    its_half = pl.ds(pl.multiple_of((1 - core) * 2 * GROUP, 2 * GROUP), 2 * GROUP)
    mine_total = other_total = None

    def project(half, columns):
        total = None
        for q, pair in enumerate(split(half)):
            for part in range(2):
                at = ((2 * half + q) * 2 + part) * NB
                term = dot(pair[part], stored[at : at + NB, columns])
                total = term if total is None else total + term
        return total

    def spread(coef, half, columns):
        coef = coef.astype(BF16)
        parts = []
        for site in (2 * half, 2 * half + 1):
            at = site * 2 * NB
            real = dot_t(coef, stored[at : at + NB, columns])
            imag = dot_t(coef, stored[at + NB : at + 2 * NB, columns])
            parts.append(real - turn(imag))
        return jnp.concatenate(parts, axis=0)

    final = []
    theirs = project(0, its_half) + project(1, its_half)
    for n in range(2):
        asend[n] = theirs
        cross = remote(asend.at[n], arecv.at[n], as_sem.at[n], ar_sem.at[n], partner)
        cross.start()
        mine = project(0, my_half) + project(1, my_half)
        cross.wait_recv()
        mine = mine + arecv[n]
        zbuf[n, chip] = jnp.concatenate(
            [mine[:, :GROUP], mine[:, GROUP:]], axis=0
        ).astype(BF16)
        sends = []
        for j in (8, 7, 9, 6, 10, 5, 11, 4, 12, 3, 13, 2, 14, 1, 15):
            sends.append(
                remote(
                    zbuf.at[n, chip], zbuf.at[n, chip], zs_sem.at[n, j], zr_sem.at[n, chip],
                    (other_chip(j) * 2 + core, kry),
                )
            )
        for send in sends:
            send.start()
        for j in range(1, CHIPS):
            source = other_chip(j)
            remote(
                zbuf.at[n, source], zbuf.at[n, source], zs_sem.at[n, j], zr_sem.at[n, source],
                (other_chip(j) * 2 + core, kry),
            ).wait_recv()
        summed = zbuf[n, 0].astype(F32)
        for q in range(1, CHIPS):
            summed = summed + zbuf[n, q].astype(F32)
        own = jnp.concatenate([summed[:ROWS], summed[ROWS:]], axis=1)
        dsend[n] = own
        cross_back = remote(dsend.at[n], drecv.at[n], ds_sem.at[n], dr_sem.at[n], partner)
        cross_back.start()
        change = [spread(own, half, my_half) for half in range(2)]
        cross_back.wait_recv()
        other = drecv[n]
        mine_total = own if n == 0 else mine_total + own
        other_total = other if n == 0 else other_total + other
        if n == 1:
            low = jnp.where(even, mine_total, other_total)
            high = jnp.where(even, other_total, mine_total)
            ebuf[0, 0], ebuf[0, 1] = low[:, :GROUP], low[:, GROUP:]
            ebuf[0, 2], ebuf[0, 3] = high[:, :GROUP], high[:, GROUP:]
            coef_sends = [
                remote(
                    ebuf.at[0, j], ebuf.at[1, y], es_sem.at[j - 1], er_sem.at[j - 1],
                    along_y(4 - j),
                )
                for j in (1, 2, 3)
            ]
            for send in coef_sends:
                send.start()
        pairs = []
        for half in range(2):
            at = halves[half]
            ssend[n, at] = (change[half] + spread(other, half, its_half)).astype(BF16)
            pair = remote(
                ssend.at[n, at], srecv.at[n, at], ss_sem.at[n, half], sr_sem.at[n, half], sibling
            )
            pair.start()
            pairs.append(pair)
        for half in range(2):
            at = halves[half]
            pairs[half].wait_recv()
            cur[at] = cur[at] - (ssend[n, at].astype(F32) + srecv[n, at].astype(F32))
            if n == 0:
                term = project(half, its_half)
                theirs = term if half == 0 else theirs + term
            else:
                fbuf[y, at] = cur[at].astype(BF16)
                for j in (2, 1, 3):
                    send = remote(
                        fbuf.at[y, at], fbuf.at[y, at],
                        fs_sem.at[j - 1, half], fr_sem.at[j - 1, half], along_y(j),
                    )
                    send.start()
                    final.append(send)
        cross.wait_send()
        for send in sends:
            send.wait_send()
        cross_back.wait_send()
        for pair in pairs:
            pair.wait_send()

    ebuf[1, y] = ebuf[0, 0]
    for j in (1, 2, 3):
        source = ring(j)
        remote(
            ebuf.at[0, j], ebuf.at[1, source], es_sem.at[j - 1], er_sem.at[j - 1], along_y(4 - j)
        ).wait()
    for part in range(2):
        rows = slice(part * QUARTER, (part + 1) * QUARTER)
        coef_ref[part] = jnp.concatenate([ebuf[1, q, rows] for q in range(4)], axis=0)
    for j in (1, 2, 3):
        source = ring(4 - j)
        for half in range(2):
            at = halves[half]
            remote(
                fbuf.at[source, at], fbuf.at[source, at],
                fs_sem.at[j - 1, half], fr_sem.at[j - 1, half], along_y(j),
            ).wait_recv()
    for send in final:
        send.wait_send()
    out_ref[...] = fbuf[...]


def shards(start_block, self_block, hop_links, stored_vectors):
    flat = jnp.transpose(stored_vectors.reshape(GROUP, FLAT))
    vmem, anywhere = pltpu.VMEM, pl.BlockSpec(memory_space=pltpu.HBM)
    here = pl.BlockSpec(memory_space=vmem)
    dma, block = pltpu.SemaphoreType.DMA, (SITES * ROWS, NB)
    out, coef = pl.pallas_call(
        kernel,
        out_shape=(
            jax.ShapeDtypeStruct((4,) + block, BF16),
            jax.ShapeDtypeStruct((2, 16, GROUP), F32),
        ),
        in_specs=[anywhere] * 4,
        out_specs=(here, here),
        scratch_shapes=[
            vmem((SITES, QUARTER, 2, NB), BF16),
            vmem((SITES, 2, NB, NB), BF16),
            vmem((SITES, 2, NB, NB), BF16),
            vmem((SITES, 2, NB, NB), BF16),
            vmem((SITES, 2, NB, NB), BF16),
            vmem((SITES, 2, NB, NB), BF16),
            vmem((FLAT, 4 * GROUP), BF16),
            vmem(block, F32),
            vmem(block, F32),
            vmem(block, F32),
            vmem(block, F32),
            vmem(block, BF16),
            vmem((3,) + block, BF16),
            vmem((2,) + block, BF16),
            vmem((3,) + block, BF16),
            vmem((2, ROWS, 2 * GROUP), F32),
            vmem((2, ROWS, 2 * GROUP), F32),
            vmem((2, CHIPS, 2 * ROWS, GROUP), BF16),
            vmem((2, ROWS, 2 * GROUP), F32),
            vmem((2, ROWS, 2 * GROUP), F32),
            vmem((2,) + block, BF16),
            vmem((2,) + block, BF16),
            vmem((4,) + block, BF16),
            vmem((2, 4, ROWS, GROUP), F32),
            dma((3 * SITES + 2,)),
            dma((2,)), dma((3, 2)), dma((2, 2)), dma((3, 2)),
            dma((3,)), dma((3,)),
            dma((2,)), dma((2,)),
            dma((2, CHIPS)), dma((2, CHIPS)),
            dma((2,)), dma((2,)), dma((2, 2)), dma((2, 2)),
            dma((3, 2)), dma((3, 2)), dma((3,)), dma((3,)),
            pltpu.SemaphoreType.REGULAR((4, 2)),
        ],
        compiler_params=pltpu.CompilerParams(
            collective_id=0, has_side_effects=True, vmem_limit_bytes=55000 * 2**10
        ),
    )(start_block[0], self_block[0], hop_links[0], flat)
    out = out.reshape(4, SITES, 2, QUARTER, NB)
    out = jnp.transpose(out, (1, 0, 3, 2, 4)).reshape(1, SITES, 16, 2, NB)
    return out, jnp.transpose(coef, (2, 0, 1))


def solution(mesh):
    placed = (
        P("lat", None, None, None, None),
        P("lat", None, None, None, None),
        P("lat", None, None, None, None, None),
        P("krylov", "lat", None, None, None),
    )
    return jax.shard_map(
        shards,
        mesh=mesh,
        in_specs=placed,
        out_specs=(P("lat", None, None, None, None), P("krylov", None, None)),
        check_vma=False,
    )
```

```python
import functools

import jax
import jax.numpy as jnp
from jax import lax
from jax.experimental import pallas as pl
from jax.experimental.pallas import tpu as pltpu
from jax.sharding import PartitionSpec as P

MESH = pl.DeviceIdType.MESH
BF16, F32 = jnp.bfloat16, jnp.float32

DEG = 6
CENTER = 0.25
HALF_WIDTH = 3.25

SITES, NB = 4, 400
QUARTER = 4
ROWS = 2 * QUARTER
FLAT = SITES * 2 * NB
GROUP = 128
CHIPS = 16


def dot(x, w):
    return lax.dot_general(x, w, (((1,), (0,)), ((), ())), preferred_element_type=F32)


def dot_t(x, w):
    return lax.dot_general(x, w, (((1,), (1,)), ((), ())), preferred_element_type=F32)


def turn(x):
    half = x.shape[0] // 2
    if x.shape[0] == ROWS:
        return jnp.concatenate([x[half:], -x[:half]], axis=0)
    return jnp.concatenate(
        [turn(x[i : i + ROWS]) for i in range(0, x.shape[0], ROWS)], axis=0
    )


def kernel(
    start_hbm, self_hbm, hop_hbm, stored_hbm,
    out_ref, coef_ref,
    start, self_w, space_w, time_w, ahead_w, beside_w, stored,
    cur, prev, acc, base, bsend, vrecv, psend, precv,
    asend, arecv, zbuf, dsend, drecv, ssend, srecv, fbuf, ebuf,
    load_sem, vs_sem, vr_sem, ps_sem, pr_sem, gs_sem, gr_sem,
    as_sem, ar_sem, zs_sem, zr_sem, ds_sem, dr_sem, ss_sem, sr_sem,
    fs_sem, fr_sem, es_sem, er_sem, word_sem,
):
    lat, kry = lax.axis_index("lat"), lax.axis_index("krylov")
    y, h = lax.rem(kry, 4), kry // 4
    core, chip = lax.rem(lat, 2), lat // 2
    ahead = (lax.rem(lat + 1, 32), kry)
    behind = (lax.rem(lat + 31, 32), kry)
    partner = (chip * 2 + 1 - core, kry)
    sibling = (lat, (1 - h) * 4 + y)

    def ring(j):
        return lax.rem(y + j, 4)

    def along_y(j):
        return (lat, h * 4 + ring(j))

    def other_chip(j):
        return lax.rem(chip + j, CHIPS)

    barrier = pltpu.get_barrier_semaphore()
    greet = [ahead, behind, sibling]
    greet += [along_y(j) for j in (1, 2, 3)]
    beside_z = [(other_chip(j) * 2 + core, kry) for j in (2, CHIPS - 2)]
    greet += beside_z
    for device in greet:
        pl.semaphore_signal(barrier, inc=1, device_id=device, device_id_type=MESH)

    def remote(src, dst, send_sem, recv_sem, device):
        return pltpu.make_async_remote_copy(
            src_ref=src, dst_ref=dst, send_sem=send_sem, recv_sem=recv_sem,
            device_id=device, device_id_type=MESH,
        )

    even, odd = core == 0, core == 1
    halves = (pl.ds(0, 2 * ROWS), pl.ds(2 * ROWS, 2 * ROWS))

    def split(half):
        x = cur[halves[half]]
        return [
            (q.astype(BF16), turn(q).astype(BF16)) for q in (x[:ROWS], x[ROWS:])
        ]

    def apply(pair, weight, site):
        return dot(pair[0], weight[site, 0]) + dot(pair[1], weight[site, 1])

    def product(half, i):
        pairs = split(half)
        psend[lax.rem(i, 2), halves[half]] = jnp.concatenate(
            [apply(pairs[q], time_w, 2 * half + q) for q in range(2)], axis=0
        ).astype(BF16)

    first_load = pltpu.make_async_copy(
        start_hbm.at[:, pl.ds(y * QUARTER, QUARTER)], start, load_sem.at[3 * SITES]
    )
    last_load = pltpu.make_async_copy(
        stored_hbm, stored.at[:, pl.ds(0, GROUP)], load_sem.at[3 * SITES + 1]
    )
    time_loads = [
        pltpu.make_async_copy(hop_hbm.at[q, 1], time_w.at[q], load_sem.at[q])
        for q in range(SITES)
    ]
    space_loads = [
        pltpu.make_async_copy(hop_hbm.at[q, 0], space_w.at[q], load_sem.at[SITES + q])
        for q in range(SITES)
    ]
    self_loads = [
        pltpu.make_async_copy(self_hbm.at[q], self_w.at[q], load_sem.at[2 * SITES + q])
        for q in range(SITES)
    ]
    for load in [first_load] + time_loads + space_loads + self_loads + [last_load]:
        load.start()
    first_load.wait()
    block = start[...].astype(F32)
    block = jnp.concatenate(
        [block[s, r, c : c + 1] for s in range(SITES) for c in range(2) for r in range(QUARTER)],
        axis=0,
    )
    cur[...] = block
    prev[...] = block
    psend[1] = jnp.zeros_like(psend[1])
    def unit(n):
        row = lax.broadcasted_iota(jnp.int32, (n, n), 0)
        return (row == lax.broadcasted_iota(jnp.int32, (n, n), 1)).astype(BF16)

    def flip(weight, flipped, site):
        source = weight[site, 0]
        flipped[site, 0] = jnp.concatenate(
            [dot_t(unit(256), source[:, :256]), dot_t(unit(144), source[:, 256:])], axis=0
        ).astype(BF16)
        flipped[site, 1] = -jnp.transpose(weight[site, 1])

    for site in range(SITES):
        time_loads[site].wait()
        if site % 2:
            product(site // 2, 0)
        flip(time_w, ahead_w, site)
    pl.semaphore_wait(barrier, len(greet))

    gathers = [
        remote(
            stored_hbm, stored.at[:, pl.ds(j * GROUP, GROUP)],
            gs_sem.at[j - 1], gr_sem.at[j - 1], along_y(j),
        )
        for j in (1, 2, 3)
    ]

    def to_behind(slot, half):
        return remote(
            bsend.at[halves[half]], vrecv.at[slot, halves[half]],
            vs_sem.at[half], vr_sem.at[slot, half], behind,
        )

    def to_ahead(parity, slot, half):
        return remote(
            psend.at[parity, halves[half]], precv.at[slot, halves[half]],
            ps_sem.at[parity, half], pr_sem.at[slot, half], ahead,
        )

    def factor(i):
        first = lax.rem(i, DEG) == 0
        return jnp.where(first, 1.0 / HALF_WIDTH, 2.0 / HALF_WIDTH).astype(F32)

    def meet(i):
        for turn_at in range(5):

            @pl.when(i == 2 * turn_at + 2)
            def _():
                if turn_at > 0:
                    pl.semaphore_wait(word_sem.at[turn_at - 1, 0], 1)
                    pl.semaphore_wait(word_sem.at[turn_at - 1, 1], 1)
                if turn_at < 4:
                    for q, device in enumerate(beside_z):
                        pl.semaphore_signal(
                            word_sem.at[turn_at, q], inc=1, device_id=device, device_id_type=MESH
                        )

    last = 2 * DEG - 1

    def put(site, value, add=True):
        at = pl.ds(site * ROWS, ROWS)
        acc[at] = acc[at] + value if add else value

    def from_first():
        zero, one = split(0)
        put(0, apply(zero, self_w, 0) + apply(one, beside_w, 0), False)
        put(1, apply(one, self_w, 1) + apply(zero, space_w, 0), False)
        put(2, apply(one, space_w, 1), False)
        put(3, apply(zero, beside_w, 3), False)

    def second_to_first():
        two, three = split(1)
        put(0, apply(three, space_w, 3))
        put(1, apply(two, beside_w, 1))

    def second_to_second():
        two, three = split(1)
        put(2, apply(two, self_w, 2) + apply(three, beside_w, 2))
        put(3, apply(three, self_w, 3) + apply(two, space_w, 2))

    def own_terms(half, i):
        at = halves[half]
        keep = jnp.where(lax.rem(i, DEG) == 0, 0.0, 1.0).astype(F32)
        return factor(i) * (acc[at] - CENTER * cur[at]) - keep * prev[at]

    def from_ahead(half, i, known):
        to_behind(lax.rem(i, 3), half).wait_recv()
        v = vrecv[lax.rem(i, 3), halves[half]].astype(F32)
        if known:
            earlier = lax.rem(i + 1, 2)
            v = v + factor(i + DEG - 1) * psend[earlier, halves[half]].astype(F32)
        pairs = [(q.astype(BF16), turn(q).astype(BF16)) for q in (v[:ROWS], v[ROWS:])]
        return factor(i) * jnp.concatenate(
            [apply(pairs[q], ahead_w, 2 * half + q) for q in range(2)], axis=0
        )

    def finish(half, i, value):
        at = halves[half]
        to_ahead(0, lax.rem(i, 3), half).wait_recv()
        value = value + factor(i) * precv[lax.rem(i, 3), at].astype(F32)
        prev[at] = cur[at]
        cur[at] = value

    def send_behind(half, slot, value):
        to_behind(slot, half).wait_send()
        bsend[halves[half]] = value.astype(BF16)
        to_behind(slot, half).start()

    def next_product(half, i):
        @pl.when(i >= 1)
        def _():
            to_ahead(lax.rem(i + 1, 2), 0, half).wait_send()

        product(half, i + 1)
        to_ahead(lax.rem(i + 1, 2), lax.rem(i + 1, 3), half).start()

    def even_step(i):
        second_to_first()
        base[halves[0]] = own_terms(0, i) + from_ahead(0, i, False)

        @pl.when(i < last)
        def _():
            send_behind(0, lax.rem(i + 1, 3), base[halves[0]])

        second_to_second()
        base[halves[1]] = own_terms(1, i) + from_ahead(1, i, False)

        @pl.when(i < last)
        def _():
            send_behind(1, lax.rem(i + 1, 3), base[halves[1]])

        finish(0, i, base[halves[0]])

        @pl.when(i < last)
        def _():
            next_product(0, i)
            from_first()

        finish(1, i, base[halves[1]])

        @pl.when(i < last)
        def _():
            next_product(1, i)

    def odd_step(i):
        from_first()
        second_to_first()
        second_to_second()
        for half in range(2):
            finish(half, i, own_terms(half, i) + from_ahead(half, i, True))

            @pl.when(i < last)
            def _(half=half):
                next_product(half, i)
                send_behind(half, lax.rem(i + 1, 3), cur[halves[half]])

    for q in (1, 0, 2):
        gathers[q].start()
    bsend[...] = cur[...].astype(BF16)
    for half in range(2):
        to_behind(0, half).start()
        to_ahead(0, 0, half).start()
    for site in range(SITES):
        space_loads[site].wait()
        flip(space_w, beside_w, site)
    for load in self_loads:
        load.wait()

    @pl.when(even)
    def _():
        from_first()

    def step(i, carry):
        meet(i)
        pl.when(even)(lambda: even_step(i))
        pl.when(odd)(lambda: odd_step(i))
        return carry

    lax.fori_loop(0, 2 * DEG, step, 0)
    for half in range(2):
        to_behind(0, half).wait_send()
        to_ahead(0, 0, half).wait_send()
        to_ahead(1, 0, half).wait_send()

    last_load.wait()
    for gather in gathers:
        gather.wait()

    my_half = pl.ds(pl.multiple_of(core * 2 * GROUP, 2 * GROUP), 2 * GROUP)
    its_half = pl.ds(pl.multiple_of((1 - core) * 2 * GROUP, 2 * GROUP), 2 * GROUP)
    mine_total = other_total = None

    def project(half, columns):
        total = None
        for q, pair in enumerate(split(half)):
            for part in range(2):
                at = ((2 * half + q) * 2 + part) * NB
                term = dot(pair[part], stored[at : at + NB, columns])
                total = term if total is None else total + term
        return total

    def spread(coef, half, columns):
        coef = coef.astype(BF16)
        parts = []
        for site in (2 * half, 2 * half + 1):
            at = site * 2 * NB
            real = dot_t(coef, stored[at : at + NB, columns])
            imag = dot_t(coef, stored[at + NB : at + 2 * NB, columns])
            parts.append(real - turn(imag))
        return jnp.concatenate(parts, axis=0)

    final = []
    theirs = project(0, its_half) + project(1, its_half)
    for n in range(2):
        asend[n] = theirs
        cross = remote(asend.at[n], arecv.at[n], as_sem.at[n], ar_sem.at[n], partner)
        cross.start()
        mine = project(0, my_half) + project(1, my_half)
        cross.wait_recv()
        mine = mine + arecv[n]
        zbuf[n, chip] = jnp.concatenate(
            [mine[:, :GROUP], mine[:, GROUP:]], axis=0
        ).astype(BF16)
        sends = []
        for j in (8, 7, 9, 6, 10, 5, 11, 4, 12, 3, 13, 2, 14, 1, 15):
            sends.append(
                remote(
                    zbuf.at[n, chip], zbuf.at[n, chip], zs_sem.at[n, j], zr_sem.at[n, chip],
                    (other_chip(j) * 2 + core, kry),
                )
            )
        for send in sends:
            send.start()
        for j in range(1, CHIPS):
            source = other_chip(j)
            remote(
                zbuf.at[n, source], zbuf.at[n, source], zs_sem.at[n, j], zr_sem.at[n, source],
                (other_chip(j) * 2 + core, kry),
            ).wait_recv()
        summed = zbuf[n, 0].astype(F32)
        for q in range(1, CHIPS):
            summed = summed + zbuf[n, q].astype(F32)
        own = jnp.concatenate([summed[:ROWS], summed[ROWS:]], axis=1)
        dsend[n] = own
        cross_back = remote(dsend.at[n], drecv.at[n], ds_sem.at[n], dr_sem.at[n], partner)
        cross_back.start()
        change = [spread(own, half, my_half) for half in range(2)]
        cross_back.wait_recv()
        other = drecv[n]
        mine_total = own if n == 0 else mine_total + own
        other_total = other if n == 0 else other_total + other
        if n == 1:
            low = jnp.where(even, mine_total, other_total)
            high = jnp.where(even, other_total, mine_total)
            ebuf[0, 0], ebuf[0, 1] = low[:, :GROUP], low[:, GROUP:]
            ebuf[0, 2], ebuf[0, 3] = high[:, :GROUP], high[:, GROUP:]
            coef_sends = [
                remote(
                    ebuf.at[0, j], ebuf.at[1, y], es_sem.at[j - 1], er_sem.at[j - 1],
                    along_y(4 - j),
                )
                for j in (1, 2, 3)
            ]
            for send in coef_sends:
                send.start()
        pairs = []
        for half in range(2):
            at = halves[half]
            ssend[n, at] = (change[half] + spread(other, half, its_half)).astype(BF16)
            pair = remote(
                ssend.at[n, at], srecv.at[n, at], ss_sem.at[n, half], sr_sem.at[n, half], sibling
            )
            pair.start()
            pairs.append(pair)
        for half in range(2):
            at = halves[half]
            pairs[half].wait_recv()
            cur[at] = cur[at] - (ssend[n, at].astype(F32) + srecv[n, at].astype(F32))
            if n == 0:
                term = project(half, its_half)
                theirs = term if half == 0 else theirs + term
            else:
                fbuf[y, at] = cur[at].astype(BF16)
                for j in (2, 1, 3):
                    send = remote(
                        fbuf.at[y, at], fbuf.at[y, at],
                        fs_sem.at[j - 1, half], fr_sem.at[j - 1, half], along_y(j),
                    )
                    send.start()
                    final.append(send)
        cross.wait_send()
        for send in sends:
            send.wait_send()
        cross_back.wait_send()
        for pair in pairs:
            pair.wait_send()

    ebuf[1, y] = ebuf[0, 0]
    for j in (1, 2, 3):
        source = ring(j)
        remote(
            ebuf.at[0, j], ebuf.at[1, source], es_sem.at[j - 1], er_sem.at[j - 1], along_y(4 - j)
        ).wait()
    for part in range(2):
        rows = slice(part * QUARTER, (part + 1) * QUARTER)
        coef_ref[part] = jnp.concatenate([ebuf[1, q, rows] for q in range(4)], axis=0)
    for j in (1, 2, 3):
        source = ring(4 - j)
        for half in range(2):
            at = halves[half]
            remote(
                fbuf.at[source, at], fbuf.at[source, at],
                fs_sem.at[j - 1, half], fr_sem.at[j - 1, half], along_y(j),
            ).wait_recv()
    for send in final:
        send.wait_send()
    out_ref[...] = fbuf[...]


def shards(start_block, self_block, hop_links, stored_vectors):
    flat = jnp.transpose(stored_vectors.reshape(GROUP, FLAT))
    vmem, anywhere = pltpu.VMEM, pl.BlockSpec(memory_space=pltpu.HBM)
    here = pl.BlockSpec(memory_space=vmem)
    dma, block = pltpu.SemaphoreType.DMA, (SITES * ROWS, NB)
    out, coef = pl.pallas_call(
        kernel,
        out_shape=(
            jax.ShapeDtypeStruct((4,) + block, BF16),
            jax.ShapeDtypeStruct((2, 16, GROUP), F32),
        ),
        in_specs=[anywhere] * 4,
        out_specs=(here, here),
        scratch_shapes=[
            vmem((SITES, QUARTER, 2, NB), BF16),
            vmem((SITES, 2, NB, NB), BF16),
            vmem((SITES, 2, NB, NB), BF16),
            vmem((SITES, 2, NB, NB), BF16),
            vmem((SITES, 2, NB, NB), BF16),
            vmem((SITES, 2, NB, NB), BF16),
            vmem((FLAT, 4 * GROUP), BF16),
            vmem(block, F32),
            vmem(block, F32),
            vmem(block, F32),
            vmem(block, F32),
            vmem(block, BF16),
            vmem((3,) + block, BF16),
            vmem((2,) + block, BF16),
            vmem((3,) + block, BF16),
            vmem((2, ROWS, 2 * GROUP), F32),
            vmem((2, ROWS, 2 * GROUP), F32),
            vmem((2, CHIPS, 2 * ROWS, GROUP), BF16),
            vmem((2, ROWS, 2 * GROUP), F32),
            vmem((2, ROWS, 2 * GROUP), F32),
            vmem((2,) + block, BF16),
            vmem((2,) + block, BF16),
            vmem((4,) + block, BF16),
            vmem((2, 4, ROWS, GROUP), F32),
            dma((3 * SITES + 2,)),
            dma((2,)), dma((3, 2)), dma((2, 2)), dma((3, 2)),
            dma((3,)), dma((3,)),
            dma((2,)), dma((2,)),
            dma((2, CHIPS)), dma((2, CHIPS)),
            dma((2,)), dma((2,)), dma((2, 2)), dma((2, 2)),
            dma((3, 2)), dma((3, 2)), dma((3,)), dma((3,)),
            pltpu.SemaphoreType.REGULAR((4, 2)),
        ],
        compiler_params=pltpu.CompilerParams(
            collective_id=0, has_side_effects=True, vmem_limit_bytes=55000 * 2**10
        ),
    )(start_block[0], self_block[0], hop_links[0], flat)
    out = out.reshape(4, SITES, 2, QUARTER, NB)
    out = jnp.transpose(out, (1, 0, 3, 2, 4)).reshape(1, SITES, 16, 2, NB)
    return out, jnp.transpose(coef, (2, 0, 1))


def solution(mesh):
    placed = (
        P("lat", None, None, None, None),
        P("lat", None, None, None, None),
        P("lat", None, None, None, None, None),
        P("krylov", "lat", None, None, None),
    )
    return jax.shard_map(
        shards,
        mesh=mesh,
        in_specs=placed,
        out_specs=(P("lat", None, None, None, None), P("krylov", None, None)),
        check_vma=False,
    )
```
